256 devices in a mesh: queue: 128 (over z, y, x), seq: 2 (over core).
Axes of the slice: x: 4, y: 4, z: 8, core: 2. Of those that a mesh axis runs over, the one named last changes fastest.
Arguments:
- latents: bfloat16 [128, 256, 3072], P('queue', 'seq'), may hold values from -6 to 6
- fresh_noise: bfloat16 [2, 256, 3072], P(None, 'seq'), may hold values from -6 to 6
- levels: int32 [128], replicated, may hold values from 0 to 49
- pattern: int32 [4, 12], replicated, may hold values 0 or 1
- entry: int32 [2], replicated, may hold values from 0 to 127
- level_scale: float32 [50, 3072], replicated, may hold values from -1.5 to 1.5
- level_shift: float32 [50, 3072], replicated, may hold values from -3 to 3
- step_size: float32 [50], replicated, may hold values from 0.2 to 1
- qk_gain: float32 [2, 64], replicated, may hold values from 0.5 to 2
- wq: bfloat16 [3072, 1536], P(None, 'seq'), may hold values from -0.109375 to 0.109375
- wk: bfloat16 [3072, 1536], P(None, 'seq'), may hold values from -0.109375 to 0.109375
- wv: bfloat16 [3072, 1536], P(None, 'seq'), may hold values from -0.109375 to 0.109375
- wo: bfloat16 [1536, 3072], P('seq'), may hold values from -0.15625 to 0.15625
Outputs:
- result: bfloat16 [128, 256, 3072], P('queue', 'seq')
The draws below stay inside these ranges and needn't reach their ends.
All inputs are finite; a program needn't handle non-finite values.
Results may differ from the reference program's by a relative error of at most 0.012.
Values may be sent and summed in bfloat16 or wider, within the bound.
No kernel may reach another device: no remote copies, remote signals or barrier semaphores. Data moves between devices by JAX's collectives and lax.ppermute only.
A program may use at most 128 MiB of HBM per device.

```python
import math
import jax
import jax.numpy as jnp
from jax import lax

D = 3072
HEADS = 24
HD = 64
FRAMES = 4
LEVELS = 50
ITERS = 2
TOK = 256
QUEUE = 128
INNER = 1536
N_SEQ = 2


def touch_ends(values, own_key, low, largest):
    shape = values.shape
    index_at = [jax.random.randint(jax.random.fold_in(own_key, axis), (), 0, shape[axis]) for axis in range(len(shape))]
    values = values.at[tuple(index_at)].set(low)
    longest = shape.index(max(shape))
    index_at[longest] = (index_at[longest] + 1) % shape[longest]
    return values.at[tuple(index_at)].set(largest)


def block_levels(stream_key, extent, split, smallest, high):
    level = 1.0
    for axis_at, blocks in split:
        steps = jax.random.uniform(jax.random.fold_in(jax.random.fold_in(stream_key, 6), axis_at), (blocks,), jnp.float32, smallest / len(split), high / len(split))
        level = level * jnp.repeat(jnp.exp(steps), extent[axis_at] // blocks).reshape((-1,) + (1,) * (len(extent) - 1 - axis_at))
    return level


def scatter_about(rng, shape, width, bound, shards=(), kind=jnp.bfloat16):
    entries = width * jax.random.normal(rng, shape, jnp.float32)
    if shards:
        entries = entries * block_levels(rng, shape, shards, -0.22, 0.18)
    return jnp.clip(entries, -bound, bound).astype(kind)


def setup_inputs(seed: int = 0) -> dict:
    arg_keys = jax.random.split(jax.random.key(seed), 14)
    latents = scatter_about(arg_keys[0], (QUEUE, TOK, D), 1.0, 6.0, ((0, 128), (1, 2)))
    fresh_noise = scatter_about(arg_keys[1], (ITERS, TOK, D), 1.0, 6.0, ((1, 2),))
    levels = touch_ends(jax.random.randint(arg_keys[2], (QUEUE,), 0, LEVELS), jax.random.fold_in(arg_keys[2], 1), 0, LEVELS - 1).astype(jnp.int32)
    pattern = touch_ends((jax.random.randint(arg_keys[3], (FRAMES, 3 * FRAMES), 0, 2) < 1).astype(jnp.int32), jax.random.fold_in(arg_keys[3], 1), 0, 1)
    entry = jax.random.randint(arg_keys[4], (ITERS,), 0, QUEUE).astype(jnp.int32)
    level_scale = scatter_about(arg_keys[5], (LEVELS, D), 0.3, 1.5, (), jnp.float32)
    level_shift = scatter_about(arg_keys[6], (LEVELS, D), 0.5, 3.0, (), jnp.float32)
    step_size = jnp.clip(jnp.exp(jax.random.uniform(arg_keys[7], (LEVELS,), jnp.float32, math.log(0.2), math.log(1.0))), 0.2, 1.0)
    qk_gain = jnp.clip(jax.random.uniform(arg_keys[8], (2, HD), jnp.float32, 0.5, 2.0), 0.5, 2.0)
    wq = scatter_about(arg_keys[9], (D, INNER), D ** -0.5, 0.109375, ((1, 2),))
    wk = scatter_about(arg_keys[10], (D, INNER), D ** -0.5, 0.109375, ((1, 2),))
    wv = scatter_about(arg_keys[11], (D, INNER), D ** -0.5, 0.109375, ((1, 2),))
    wo = scatter_about(arg_keys[12], (INNER, D), INNER ** -0.5, 0.15625, ((0, 2),))
    return dict(latents=latents, fresh_noise=fresh_noise, levels=levels, pattern=pattern, entry=entry, level_scale=level_scale, level_shift=level_shift, step_size=step_size, qk_gain=qk_gain, wq=wq, wk=wk, wv=wv, wo=wo)


def modulate(slot_state, scale_row, shift_row):
    values = slot_state.astype(jnp.float32)
    normed = values * lax.rsqrt(lax.optimization_barrier(jnp.mean(values * values, axis=-1, keepdims=True)) + 1e-06)
    return (normed * (1.0 + scale_row) + shift_row).astype(jnp.bfloat16)

def head_norm(values, gain):
    return (values * lax.rsqrt(lax.optimization_barrier(jnp.mean(values * values, axis=-1, keepdims=True)) + 1e-06) * gain).astype(jnp.bfloat16)

def allowed_keys(pattern, logical, queue_count, token_count):
    frame_tokens = token_count // FRAMES
    block_index = jnp.arange(3 * FRAMES, dtype=jnp.int32) // FRAMES
    present = (block_index == 1) | (block_index == 0) & (logical > 0) | (block_index == 2) & (logical < queue_count - 1)
    own_frame = jnp.arange(3 * FRAMES, dtype=jnp.int32)[None, :] == (FRAMES + jnp.arange(FRAMES, dtype=jnp.int32))[:, None]
    frame_table = ((pattern == 1) | own_frame) & present[None, :]
    return jnp.repeat(jnp.repeat(frame_table, frame_tokens, axis=0), frame_tokens, axis=1)

def attend(query, keys, values, allowed):
    scale = 1.0 / math.sqrt(HD)

    def one_head(operands):
        query_head, key_head, value_head = operands
        scores = jnp.dot(query_head, key_head.T, preferred_element_type=jnp.float32) * scale
        scores = jnp.where(allowed, scores, -1e+30)
        highest = lax.optimization_barrier(jnp.max(scores, axis=-1, keepdims=True))
        expo = jnp.exp(scores - highest)
        weights = (expo / lax.optimization_barrier(jnp.sum(expo, axis=-1, keepdims=True))).astype(jnp.bfloat16)
        return jnp.dot(weights, value_head, preferred_element_type=jnp.float32).astype(jnp.bfloat16)
    heads = lax.map(one_head, (query.transpose(1, 0, 2), keys.transpose(1, 0, 2), values.transpose(1, 0, 2)))
    return heads.transpose(1, 0, 2)

def reference(latents, fresh_noise, levels, pattern, entry, level_scale, level_shift, step_size, qk_gain, wq, wk, wv, wo):
    state = latents
    slots = jnp.arange(QUEUE, dtype=jnp.int32)
    for step_index in range(ITERS):

        def project(operands):
            slot_state, level_now = operands
            modulated = modulate(slot_state, level_scale[level_now], level_shift[level_now])
            query = head_norm(jnp.dot(modulated, wq, preferred_element_type=jnp.float32).reshape(TOK, HEADS, HD), qk_gain[0])
            keys = head_norm(jnp.dot(modulated, wk, preferred_element_type=jnp.float32).reshape(TOK, HEADS, HD), qk_gain[1])
            values = jnp.dot(modulated, wv, preferred_element_type=jnp.float32).astype(jnp.bfloat16).reshape(TOK, HEADS, HD)
            return (query, keys, values)
        query, keys, values = lax.map(project, (state, levels))
        blank = jnp.zeros((1, TOK, HEADS, HD), jnp.bfloat16)
        key_padded = jnp.concatenate([blank, keys, blank], axis=0)
        value_padded = jnp.concatenate([blank, values, blank], axis=0)

        def window(slot):
            key_window = lax.dynamic_slice_in_dim(key_padded, slot, 3, 0).reshape(3 * TOK, HEADS, HD)
            value_window = lax.dynamic_slice_in_dim(value_padded, slot, 3, 0).reshape(3 * TOK, HEADS, HD)
            allowed = allowed_keys(pattern, slot, QUEUE, TOK)
            return attend(query[slot], key_window, value_window, allowed)
        attended = lax.map(window, slots)

        def update(operands):
            slot_state, slot_attended, level_now = operands
            grouped = slot_attended.reshape(TOK, N_SEQ, INNER // N_SEQ).astype(jnp.float32)
            rows = wo.reshape(N_SEQ, INNER // N_SEQ, D).astype(jnp.float32)
            parts = jnp.einsum('tgc,gcd->gtd', grouped, rows)
            velocity = lax.optimization_barrier(jnp.sum(parts.astype(jnp.bfloat16).astype(jnp.float32), axis=0))
            return (slot_state.astype(jnp.float32) + step_size[level_now] * velocity).astype(jnp.bfloat16)
        updated = lax.map(update, (state, attended, levels))
        moved = jnp.roll(updated, 1, axis=0)
        state = jnp.where((slots == entry[step_index])[:, None, None], fresh_noise[step_index][None], moved)
    return state
```

```python
import math

import jax
import jax.numpy as jnp
from jax import lax
from jax.sharding import PartitionSpec as P

HD = 64
FRAMES = 4
ITERS = 2


def swap_cores(block):
    return lax.ppermute(block, "seq", [(0, 1), (1, 0)])


def modulate(slot_state, scale_row, shift_row):
    values = slot_state.astype(jnp.float32)
    normed = values * lax.rsqrt(jnp.mean(values * values, axis=-1, keepdims=True) + 1e-06)
    return (normed * (1.0 + scale_row) + shift_row).astype(jnp.bfloat16)


def head_norm(values, gain):
    return (
        values * lax.rsqrt(jnp.mean(values * values, axis=-1, keepdims=True) + 1e-06) * gain
    ).astype(jnp.bfloat16)


def frame_table(pattern, slot, count, core):
    block = jnp.arange(3 * FRAMES, dtype=jnp.int32) // FRAMES
    present = (block == 1) | (block == 0) & (slot > 0) | (block == 2) & (slot < count - 1)
    own = (
        jnp.arange(3 * FRAMES, dtype=jnp.int32)[None, :]
        == (FRAMES + jnp.arange(FRAMES, dtype=jnp.int32))[:, None]
    )
    table = ((pattern == 1) | own) & present[None, :]
    half = FRAMES // 2
    turned = table.reshape(2, half, 3, 2, half)[::-1, :, :, ::-1].reshape(FRAMES, 3 * FRAMES)
    return jnp.where(core == 0, table, turned)


def attend(query, keys, values, allowed):
    scale = 1.0 / math.sqrt(HD)

    def one_head(operands):
        query_head, key_head, value_head = operands
        scores = jnp.dot(query_head, key_head.T, preferred_element_type=jnp.float32) * scale
        scores = jnp.where(allowed, scores, -1e30)
        highest = jnp.max(scores, axis=-1, keepdims=True)
        expo = jnp.exp(scores - highest)
        weights = (expo / jnp.sum(expo, axis=-1, keepdims=True)).astype(jnp.bfloat16)
        return jnp.dot(weights, value_head, preferred_element_type=jnp.float32).astype(jnp.bfloat16)

    heads = lax.map(
        one_head, (query.transpose(1, 0, 2), keys.transpose(1, 0, 2), values.transpose(1, 0, 2))
    )
    return heads.transpose(1, 0, 2)


def on_device(
    latents, fresh_noise, levels, pattern, entry, level_scale, level_shift, step_size, qk_gain, wq, wk, wv, wo
):
    count = lax.axis_size("queue")
    place = lax.axis_index("queue")
    core = lax.axis_index("seq")
    state = latents[0]
    half, _ = state.shape
    tokens, width = 2 * half, wq.shape[1]
    heads = width // HD
    forward = [(i, (i + 1) % count) for i in range(count)]
    backward = [((i + 1) % count, i) for i in range(count)]
    for step in range(ITERS):
        slot = (place + step) % count
        level = levels[slot]
        modulated = modulate(state, level_scale[level], level_shift[level])
        whole = jnp.concatenate([modulated, swap_cores(modulated)], axis=0)
        keys = head_norm(
            jnp.dot(whole, wk, preferred_element_type=jnp.float32).reshape(tokens, heads, HD), qk_gain[1]
        )
        values = (
            jnp.dot(whole, wv, preferred_element_type=jnp.float32)
            .astype(jnp.bfloat16)
            .reshape(tokens, heads, HD)
        )
        pair = jnp.stack([keys.reshape(tokens, width), values.reshape(tokens, width)])
        before = lax.ppermute(pair, "queue", forward)
        after = lax.ppermute(pair, "queue", backward)
        query = head_norm(
            jnp.dot(whole, wq, preferred_element_type=jnp.float32).reshape(tokens, heads, HD), qk_gain[0]
        )
        window = jnp.concatenate([before, pair, after], axis=1).reshape(2, 3 * tokens, heads, HD)
        table = frame_table(pattern, slot, count, core)
        per_frame = tokens // FRAMES
        allowed = jnp.repeat(jnp.repeat(table, per_frame, axis=0), per_frame, axis=1)
        attended = attend(query, window[0], window[1], allowed).reshape(tokens, width)
        term = jnp.dot(attended, wo, preferred_element_type=jnp.float32).astype(jnp.bfloat16)
        other = swap_cores(term[half:])
        velocity = term[:half].astype(jnp.float32) + other.astype(jnp.float32)
        updated = (state.astype(jnp.float32) + step_size[level] * velocity).astype(jnp.bfloat16)
        state = jnp.where((slot + 1) % count == entry[step], fresh_noise[step], updated)
    route = [(i, (i + ITERS) % count) for i in range(count)]
    return lax.ppermute(state, "queue", route)[None]


def solution(mesh):
    return jax.shard_map(
        on_device,
        mesh=mesh,
        in_specs=(
            P("queue", "seq", None),
            P(None, "seq", None),
            P(),
            P(),
            P(),
            P(),
            P(),
            P(),
            P(),
            P(None, "seq"),
            P(None, "seq"),
            P(None, "seq"),
            P("seq", None),
        ),
        out_specs=P("queue", "seq", None),
        check_vma=False,
    )
```

```python
import math

import jax
import jax.numpy as jnp
from jax import lax
from jax.experimental import pallas as pl
from jax.experimental.pallas import tpu as pltpu
from jax.sharding import PartitionSpec as P

HD = 64
FRAMES = 4
ITERS = 2
LANES = 128
EPS = 1e-06
CLOSED = -30000.0
BLOCK = 256
OUT_BLOCK = 768
MIB = 1 << 20
F32 = jnp.float32
BF16 = jnp.bfloat16

SMEM = pl.BlockSpec(memory_space=pltpu.SMEM)
VMEM = pl.BlockSpec(memory_space=pltpu.VMEM)
ANY = pl.BlockSpec(memory_space=pl.ANY)


def swap_cores(block):
    return lax.ppermute(block, "seq", [(0, 1), (1, 0)])


def params(mib):
    return pltpu.CompilerParams(vmem_limit_bytes=mib * MIB)


def slot_of(step):
    return lax.rem(lax.axis_index("queue") + step, lax.axis_size("queue"))


def modulated_rows(values, scale_row, shift_row):
    normed = values * lax.rsqrt(jnp.mean(values * values, axis=-1, keepdims=True) + EPS)
    return (normed * (1.0 + scale_row) + shift_row).astype(BF16)


def modulate(state, levels, level_scale, level_shift):
    def kernel(levels_ref, state_ref, scale_ref, shift_ref, out_ref):
        row = pl.ds(levels_ref[slot_of(0)], 1)
        out_ref[...] = modulated_rows(state_ref[...].astype(F32), scale_ref[row, :], shift_ref[row, :])

    return pl.pallas_call(
        kernel,
        out_shape=jax.ShapeDtypeStruct(state.shape, BF16),
        in_specs=[SMEM, VMEM, VMEM, VMEM],
        out_specs=VMEM,
        compiler_params=params(16),
    )(levels, state, level_scale, level_shift)


def head_normed(values, gain_row):
    width = values.shape[1]
    squares = values * values
    high = squares.astype(BF16)
    low = (squares - high.astype(F32)).astype(BF16)
    row = lax.broadcasted_iota(jnp.int32, (2 * width, width), 0)
    column = lax.broadcasted_iota(jnp.int32, (2 * width, width), 1)
    row = jnp.where(row >= width, row - width, row)
    same = (row // HD == column // HD).astype(BF16)
    sums = jnp.dot(jnp.concatenate([high, low], axis=1), same, preferred_element_type=F32)
    return values * lax.rsqrt(sums * (1.0 / HD) + EPS) * gain_row


def keys_values(mine, other, qk_gain, wk, wv):
    half, depth = mine.shape
    width = wk.shape[1]
    blocks = width // BLOCK

    def kernel(gain_ref, mine_ref, other_ref, wk_ref, wv_ref, out_ref, whole):
        step = pl.program_id(0)

        @pl.when(step == 0)
        def _():
            whole[:half, :] = mine_ref[...]
            whole[half:, :] = other_ref[...]

        @pl.when(step < blocks)
        def _():
            keys = jnp.dot(whole[...], wk_ref[...], preferred_element_type=F32)
            gain = jnp.concatenate([gain_ref[1:2, :]] * (BLOCK // HD), axis=1)
            out_ref[0] = head_normed(keys, gain).astype(BF16)

        @pl.when(step >= blocks)
        def _():
            out_ref[0] = jnp.dot(whole[...], wv_ref[...], preferred_element_type=F32).astype(BF16)

    return pl.pallas_call(
        kernel,
        grid=(2 * blocks,),
        out_shape=jax.ShapeDtypeStruct((2, 2 * half, width), BF16),
        in_specs=[
            pl.BlockSpec((2, HD), lambda i: (0, 0)),
            pl.BlockSpec((half, depth), lambda i: (0, 0)),
            pl.BlockSpec((half, depth), lambda i: (0, 0)),
            pl.BlockSpec((depth, BLOCK), lambda i: (0, jnp.minimum(i, blocks - 1))),
            pl.BlockSpec((depth, BLOCK), lambda i: (0, jnp.maximum(i - blocks, 0))),
        ],
        out_specs=pl.BlockSpec((1, 2 * half, BLOCK), lambda i: (i // blocks, 0, i % blocks)),
        scratch_shapes=[pltpu.VMEM((2 * half, depth), BF16)],
        compiler_params=params(32),
    )(qk_gain, mine, other, wk, wv)


def queries(mine, other, qk_gain, wq):
    half, depth = mine.shape
    width = wq.shape[1]
    blocks = width // BLOCK
    scale = math.log2(math.e) / math.sqrt(HD)

    def kernel(gain_ref, mine_ref, other_ref, wq_ref, out_ref, whole):
        @pl.when(pl.program_id(0) == 0)
        def _():
            whole[:half, :] = mine_ref[...]
            whole[half:, :] = other_ref[...]

        query = jnp.dot(whole[...], wq_ref[...], preferred_element_type=F32)
        gain = jnp.concatenate([gain_ref[0:1, :] * scale] * (BLOCK // HD), axis=1)
        out_ref[...] = head_normed(query, gain).astype(BF16)

    return pl.pallas_call(
        kernel,
        grid=(blocks,),
        out_shape=jax.ShapeDtypeStruct((2 * half, width), BF16),
        in_specs=[
            pl.BlockSpec((2, HD), lambda i: (0, 0)),
            pl.BlockSpec((half, depth), lambda i: (0, 0)),
            pl.BlockSpec((half, depth), lambda i: (0, 0)),
            pl.BlockSpec((depth, BLOCK), lambda i: (0, i)),
        ],
        out_specs=pl.BlockSpec((2 * half, BLOCK), lambda i: (0, i)),
        scratch_shapes=[pltpu.VMEM((2 * half, depth), BF16)],
        compiler_params=params(32),
    )(qk_gain, mine, other, wq)


def window_bias(pattern_ref, bias_ref, slot, count, core, frame_rows):
    lane = lax.broadcasted_iota(jnp.int32, (1, LANES), 1)
    half = FRAMES // 2
    for block in range(3):
        absent = (slot == 0) if block == 0 else (slot == count - 1)
        for at in range(FRAMES):
            key_frame = lax.rem(at + half * core, FRAMES)
            row = jnp.zeros((1, LANES), F32)
            for f in range(FRAMES):
                if block == 1 and f == at:
                    continue
                closed = pattern_ref[lax.rem(f + half * core, FRAMES), block * FRAMES + key_frame] != 1
                if block != 1:
                    closed = jnp.logical_or(closed, absent)
                row = row + jnp.where(lane == f, jnp.where(closed, CLOSED, 0.0), 0.0)
            first = (block * FRAMES + at) * frame_rows
            bias_ref[first : first + frame_rows, :] = jnp.broadcast_to(row, (frame_rows, LANES)).astype(BF16)


def attend_project(step, query, before, own, after, pattern, wo):
    tokens, width = query.shape
    half = tokens // 2
    out_width = wo.shape[1]
    pairs = width // LANES

    def kernel(pattern_ref, query_ref, before_ref, own_ref, after_ref, wo_ref, keep_ref, send_ref, bias, key_all, value_all, attended, wo_all, sem):
        copy = pltpu.make_async_copy(wo_ref, wo_all, sem)
        copy.start()
        window_bias(
            pattern_ref, bias, slot_of(step), lax.axis_size("queue"), lax.axis_index("seq"), tokens // FRAMES
        )
        lane = lax.broadcasted_iota(jnp.int32, (tokens, LANES), 1)
        frame = lax.broadcasted_iota(jnp.int32, (tokens, LANES), 0) // (tokens // FRAMES)
        frame_of = (lane == frame).astype(BF16)
        first = lane < HD
        key_all[:, LANES:] = bias[...]
        value_all[:, LANES:] = jnp.ones((3 * tokens, LANES), BF16)
        for pair in range(pairs):
            columns = slice(pair * LANES, (pair + 1) * LANES)
            for i, ref in enumerate((before_ref, own_ref, after_ref)):
                rows = slice(i * tokens, (i + 1) * tokens)
                key_all[rows, :LANES] = ref[0, :, columns]
                value_all[rows, :LANES] = ref[1, :, columns]
            query_pair = query_ref[:, columns]
            outs = []
            for which in (first, jnp.logical_not(first)):
                one = jnp.where(which, query_pair, jnp.zeros_like(query_pair))
                one = jnp.concatenate([one, frame_of], axis=1)
                scores = lax.dot_general(
                    one, key_all[...], (((1,), (1,)), ((), ())), preferred_element_type=F32
                )
                weights = jnp.exp2(scores).astype(BF16)
                both = jnp.dot(weights, value_all[...], preferred_element_type=F32)
                outs.append(both[:, :LANES] / both[:, LANES:])
            attended[:, columns] = jnp.where(first, outs[0], outs[1]).astype(BF16)
        copy.wait()
        for block in range(out_width // OUT_BLOCK):
            columns = slice(block * OUT_BLOCK, (block + 1) * OUT_BLOCK)
            term = jnp.dot(attended[...], wo_all[:, columns], preferred_element_type=F32).astype(BF16)
            keep_ref[:, columns] = term[:half]
            send_ref[:, columns] = term[half:]

    out = jax.ShapeDtypeStruct((half, out_width), BF16)
    return pl.pallas_call(
        kernel,
        out_shape=(out, out),
        in_specs=[SMEM, VMEM, VMEM, VMEM, VMEM, ANY],
        out_specs=(VMEM, VMEM),
        scratch_shapes=[
            pltpu.VMEM((3 * tokens, LANES), BF16),
            pltpu.VMEM((3 * tokens, 2 * LANES), BF16),
            pltpu.VMEM((3 * tokens, 2 * LANES), BF16),
            pltpu.VMEM((tokens, width), BF16),
            pltpu.VMEM(wo.shape, BF16),
            pltpu.SemaphoreType.DMA(()),
        ],
        compiler_params=params(40),
    )(pattern, query, before, own, after, wo)


def update(step, state, kept, received, fresh_noise, levels, entry, step_size, level_scale, level_shift):
    last = step == ITERS - 1

    def kernel(levels_ref, entry_ref, size_ref, state_ref, kept_ref, received_ref, noise_ref, scale_ref, shift_ref, *rest):
        out_ref, sem = rest[0], rest[-1]
        count = lax.axis_size("queue")
        slot = slot_of(step)
        next_slot = lax.rem(slot + 1, count)
        velocity = kept_ref[...].astype(F32) + received_ref[...].astype(F32)
        out_ref[...] = (state_ref[...].astype(F32) + size_ref[levels_ref[slot]] * velocity).astype(BF16)

        @pl.when(next_slot == entry_ref[step])
        def _():
            copy = pltpu.make_async_copy(noise_ref.at[step], out_ref, sem)
            copy.start()
            copy.wait()

        if not last:
            row = pl.ds(levels_ref[next_slot], 1)
            rest[1][...] = modulated_rows(out_ref[...].astype(F32), scale_ref[row, :], shift_ref[row, :])

    out = jax.ShapeDtypeStruct(state.shape, BF16)
    return pl.pallas_call(
        kernel,
        out_shape=(out,) if last else (out, out),
        in_specs=[SMEM, SMEM, SMEM, VMEM, VMEM, VMEM, ANY, VMEM, VMEM],
        out_specs=(VMEM,) if last else (VMEM, VMEM),
        scratch_shapes=[pltpu.SemaphoreType.DMA(())],
        compiler_params=params(24),
    )(levels, entry, step_size, state, kept, received, fresh_noise, level_scale, level_shift)


def on_device(
    latents, fresh_noise, levels, pattern, entry, level_scale, level_shift, step_size, qk_gain, wq, wk, wv, wo
):
    count = lax.axis_size("queue")
    forward = [(i, (i + 1) % count) for i in range(count)]
    backward = [((i + 1) % count, i) for i in range(count)]
    state = latents[0]
    modulated = modulate(state, levels, level_scale, level_shift)
    for step in range(ITERS):
        other = swap_cores(modulated)
        own = keys_values(modulated, other, qk_gain, wk, wv)
        before = lax.ppermute(own, "queue", forward)
        after = lax.ppermute(own, "queue", backward)
        query = queries(modulated, other, qk_gain, wq)
        kept, sent = attend_project(step, query, before, own, after, pattern, wo)
        received = swap_cores(sent)
        state, *rest = update(
            step, state, kept, received, fresh_noise, levels, entry, step_size, level_scale, level_shift
        )
        if rest:
            modulated = rest[0]
    route = [(i, (i + ITERS) % count) for i in range(count)]
    return lax.ppermute(state, "queue", route)[None]


def solution(mesh):
    return jax.shard_map(
        on_device,
        mesh=mesh,
        in_specs=(
            P("queue", "seq", None),
            P(None, "seq", None),
            P(),
            P(),
            P(),
            P(),
            P(),
            P(),
            P(),
            P(None, "seq"),
            P(None, "seq"),
            P(None, "seq"),
            P("seq", None),
        ),
        out_specs=P("queue", "seq", None),
        check_vma=False,
    )
```

```python
import math

import jax
import jax.numpy as jnp
from jax import lax
from jax.experimental import pallas as pl
from jax.experimental.pallas import tpu as pltpu
from jax.sharding import PartitionSpec as P

HD = 64
FRAMES = 4
ITERS = 2
LANES = 128
EPS = 1e-06
CLOSED = -30000.0
BLOCK = 256
OUT_BLOCK = 768
MIB = 1 << 20
F32 = jnp.float32
BF16 = jnp.bfloat16

SMEM = pl.BlockSpec(memory_space=pltpu.SMEM)
VMEM = pl.BlockSpec(memory_space=pltpu.VMEM)
HBM = pl.BlockSpec(memory_space=pltpu.HBM)


def swap_cores(block):
    return lax.ppermute(block, "seq", [(0, 1), (1, 0)])


def in_hbm(*arrays):
    return tuple(pltpu.with_memory_space_constraint(array, pltpu.HBM) for array in arrays)


def params(mib):
    return pltpu.CompilerParams(vmem_limit_bytes=mib * MIB)


def slot_of(step):
    return lax.rem(lax.axis_index("queue") + step, lax.axis_size("queue"))


def modulated_rows(values, scale_row, shift_row):
    normed = values * lax.rsqrt(jnp.mean(values * values, axis=-1, keepdims=True) + EPS)
    return (normed * scale_row + shift_row).astype(BF16)


def head_normed(values, gain_row):
    width = values.shape[1]
    squares = values * values
    high = squares.astype(BF16)
    low = (squares - high.astype(F32)).astype(BF16)
    row = lax.broadcasted_iota(jnp.int32, (2 * width, width), 0)
    column = lax.broadcasted_iota(jnp.int32, (2 * width, width), 1)
    row = jnp.where(row >= width, row - width, row)
    same = (row // HD == column // HD).astype(BF16)
    sums = jnp.dot(jnp.concatenate([high, low], axis=1), same, preferred_element_type=F32)
    return values * lax.rsqrt(sums * (1.0 / HD) + EPS) * gain_row


def window_bias(pattern_ref, bias_ref, slot, frame_rows):
    count, core = lax.axis_size("queue"), lax.axis_index("seq")
    lane = lax.broadcasted_iota(jnp.int32, (1, LANES), 1)
    half = FRAMES // 2
    for block in range(3):
        absent = (slot == 0) if block == 0 else (slot == count - 1)
        for at in range(FRAMES):
            key_frame = lax.rem(at + half * core, FRAMES)
            row = jnp.zeros((1, LANES), F32)
            for f in range(FRAMES):
                if block == 1 and f == at:
                    continue
                closed = pattern_ref[lax.rem(f + half * core, FRAMES), block * FRAMES + key_frame] != 1
                if block != 1:
                    closed = jnp.logical_or(closed, absent)
                row = row + jnp.where(lane == f, jnp.where(closed, CLOSED, 0.0), 0.0)
            first = at * frame_rows
            bias_ref[block, first : first + frame_rows, :] = jnp.broadcast_to(row, (frame_rows, LANES)).astype(BF16)


def prepare(levels, level_scale, level_shift, wk, wv):
    depth = level_scale.shape[1]

    def kernel(levels_ref, scale_ref, shift_ref, wk_ref, wv_ref, rows_ref, wk_out, wv_out, held, levels_sm, sems):
        first = pltpu.make_async_copy(levels_ref, levels_sm, sems.at[0])
        first.start()
        weights = [
            pltpu.make_async_copy(wk_ref, wk_out, sems.at[1]),
            pltpu.make_async_copy(wv_ref, wv_out, sems.at[2]),
        ]
        tables = [
            pltpu.make_async_copy(scale_ref, held.at[0], sems.at[3]),
            pltpu.make_async_copy(shift_ref, held.at[1], sems.at[4]),
        ]
        for copy in tables + weights:
            copy.start()
        for copy in [first] + tables:
            copy.wait()
        for step in range(ITERS):
            row = pl.ds(levels_sm[slot_of(step)], 1)
            rows_ref[step, 0:1, :] = 1.0 + held[0, row, :]
            rows_ref[step, 1:2, :] = held[1, row, :]
        for copy in weights:
            copy.wait()

    return pl.pallas_call(
        kernel,
        out_shape=(
            jax.ShapeDtypeStruct((ITERS, 2, depth), F32),
            jax.ShapeDtypeStruct(wk.shape, BF16),
            jax.ShapeDtypeStruct(wv.shape, BF16),
        ),
        in_specs=[HBM] * 5,
        out_specs=(VMEM,) * 3,
        scratch_shapes=[
            pltpu.VMEM((2, *level_scale.shape), F32),
            pltpu.SMEM(levels.shape, jnp.int32),
            pltpu.SemaphoreType.DMA((5,)),
        ],
        compiler_params=params(8),
    )(*in_hbm(levels, level_scale, level_shift, wk, wv))


def project(step, whole, gain_ref, wk_ref, wv_ref, out_ref):
    width = wk_ref.shape[1]
    gain = jnp.concatenate([gain_ref[1:2, :]] * (BLOCK // HD), axis=1)
    for block in range(width // BLOCK):
        columns = slice(block * BLOCK, (block + 1) * BLOCK)
        keys = jnp.dot(whole[...], wk_ref[:, columns], preferred_element_type=F32)
        out_ref[0, :, columns] = head_normed(keys, gain).astype(BF16)
        values = jnp.dot(whole[...], wv_ref[:, columns], preferred_element_type=F32)
        out_ref[1, :, columns] = values.astype(BF16)


def first_keys_values(mine, other, rows, qk_gain, wk, wv):
    half, depth = mine.shape
    width = wk.shape[1]

    def kernel(mine_ref, other_ref, rows_ref, gain_ref, wk_ref, wv_ref, whole, out_ref):
        scale_row, shift_row = rows_ref[0, 0:1, :], rows_ref[0, 1:2, :]
        whole[:half, :] = modulated_rows(mine_ref[...].astype(F32), scale_row, shift_row)
        whole[half:, :] = modulated_rows(other_ref[...].astype(F32), scale_row, shift_row)
        project(0, whole, gain_ref, wk_ref, wv_ref, out_ref)

    return pl.pallas_call(
        kernel,
        out_shape=(
            jax.ShapeDtypeStruct((2 * half, depth), BF16),
            jax.ShapeDtypeStruct((2, 2 * half, width), BF16),
        ),
        in_specs=[VMEM] * 6,
        out_specs=(VMEM, VMEM),
        compiler_params=params(8),
    )(mine, other, rows, qk_gain, wk, wv)


def next_keys_values(step, mine, other, terms, received, rows, qk_gain, wk, wv, levels, entry, step_size):
    half, depth = mine.shape
    width = wk.shape[1]

    def kernel(levels_ref, entry_ref, size_ref, mine_ref, other_ref, term_mine, term_other, their_own, their_mine, rows_ref, gain_ref, wk_ref, wv_ref, state_ref, whole, out_ref):
        slot = slot_of(step - 1)
        fresh = slot_of(step) == entry_ref[step - 1]
        size = size_ref[levels_ref[slot]]
        scale_row, shift_row = rows_ref[step, 0:1, :], rows_ref[step, 1:2, :]

        def moved(state, term_a, term_b, noise):
            velocity = term_a[...].astype(F32) + term_b[...].astype(F32)
            updated = (state[...].astype(F32) + size * velocity).astype(BF16)
            return jnp.where(fresh, noise[...], updated)

        new = moved(mine_ref, term_mine, their_mine, term_mine)
        state_ref[...] = new
        whole[:half, :] = modulated_rows(new.astype(F32), scale_row, shift_row)
        new = moved(other_ref, term_other, their_own, their_own)
        whole[half:, :] = modulated_rows(new.astype(F32), scale_row, shift_row)
        project(step, whole, gain_ref, wk_ref, wv_ref, out_ref)

    return pl.pallas_call(
        kernel,
        out_shape=(
            jax.ShapeDtypeStruct((half, depth), BF16),
            jax.ShapeDtypeStruct((2 * half, depth), BF16),
            jax.ShapeDtypeStruct((2, 2 * half, width), BF16),
        ),
        in_specs=[SMEM] * 3 + [VMEM] * 10,
        out_specs=(VMEM,) * 3,
        compiler_params=params(8),
    )(levels, entry, step_size, mine, other, *terms, *received, rows, qk_gain, wk, wv)


def queries(step, whole, qk_gain, wq, pattern):
    tokens = whole.shape[0]
    width = wq.shape[1]
    scale = math.log2(math.e) / math.sqrt(HD)

    def kernel(pattern_ref, gain_ref, whole_ref, wq_ref, out_ref, bias_ref):
        window_bias(pattern_ref, bias_ref, slot_of(step), tokens // FRAMES)
        gain = jnp.concatenate([gain_ref[0:1, :] * scale] * (BLOCK // HD), axis=1)
        for block in range(width // BLOCK):
            columns = slice(block * BLOCK, (block + 1) * BLOCK)
            query = jnp.dot(whole_ref[...], wq_ref[:, columns], preferred_element_type=F32)
            out_ref[:, columns] = head_normed(query, gain).astype(BF16)

    return pl.pallas_call(
        kernel,
        out_shape=(
            jax.ShapeDtypeStruct((tokens, width), BF16),
            jax.ShapeDtypeStruct((3, tokens, LANES), BF16),
        ),
        in_specs=[SMEM, VMEM, VMEM, VMEM],
        out_specs=(VMEM, VMEM),
        compiler_params=params(8),
    )(pattern, qk_gain, whole, wq)


def attend_project(step, query, bias, before, own, after, wo, fresh_noise, entry):
    tokens, width = query.shape
    half = tokens // 2
    out_width = wo.shape[1]
    last = step == ITERS - 1

    def kernel(entry_ref, query_ref, bias_ref, before_ref, own_ref, after_ref, wo_ref, noise_ref, keep_ref, send_ref, attended, sem):
        lane = lax.broadcasted_iota(jnp.int32, (tokens, LANES), 1)
        frame = lax.broadcasted_iota(jnp.int32, (tokens, LANES), 0) // (tokens // FRAMES)
        frame_of = (lane == frame).astype(BF16)
        first = lane < HD
        ones = jnp.ones((tokens, LANES), BF16)
        for pair in range(width // LANES):
            columns = slice(pair * LANES, (pair + 1) * LANES)
            query_pair = query_ref[:, columns]
            outs = []
            for which in (first, jnp.logical_not(first)):
                one = jnp.where(which, query_pair, jnp.zeros_like(query_pair))
                one = jnp.concatenate([one, frame_of], axis=1)
                both = None
                for i, ref in enumerate((before_ref, own_ref, after_ref)):
                    key = jnp.concatenate([ref[0, :, columns], bias_ref[i]], axis=1)
                    value = jnp.concatenate([ref[1, :, columns], ones], axis=1)
                    scores = lax.dot_general(one, key, (((1,), (1,)), ((), ())), preferred_element_type=F32)
                    weights = jnp.exp2(scores).astype(BF16)
                    part = jnp.dot(weights, value, preferred_element_type=F32)
                    both = part if both is None else both + part
                outs.append(both[:, :LANES] / both[:, LANES:])
            attended[:, columns] = jnp.where(first, outs[0], outs[1]).astype(BF16)
        for block in range(out_width // OUT_BLOCK):
            columns = slice(block * OUT_BLOCK, (block + 1) * OUT_BLOCK)
            term = jnp.dot(attended[...], wo_ref[:, columns], preferred_element_type=F32).astype(BF16)
            keep_ref[:, columns] = term[:half]
            send_ref[:, columns] = term[half:]
        if not last:

            @pl.when(slot_of(step + 1) == entry_ref[step])
            def _():
                copy = pltpu.make_async_copy(noise_ref.at[step], keep_ref, sem)
                copy.start()
                copy.wait()

    out = jax.ShapeDtypeStruct((half, out_width), BF16)
    return pl.pallas_call(
        kernel,
        out_shape=(out, out),
        in_specs=[SMEM, VMEM, VMEM, VMEM, VMEM, VMEM, VMEM, HBM],
        out_specs=(VMEM, VMEM),
        scratch_shapes=[pltpu.VMEM((tokens, width), BF16), pltpu.SemaphoreType.DMA(())],
        compiler_params=params(8),
    )(entry, query, bias, before, own, after, wo, *in_hbm(fresh_noise))


def last_update(state, kept, received, fresh_noise, levels, entry, step_size):
    step = ITERS - 1

    def kernel(levels_ref, entry_ref, size_ref, state_ref, kept_ref, received_ref, noise_ref, out_ref, sem):
        velocity = kept_ref[...].astype(F32) + received_ref[...].astype(F32)
        size = size_ref[levels_ref[slot_of(step)]]
        out_ref[...] = (state_ref[...].astype(F32) + size * velocity).astype(BF16)

        @pl.when(slot_of(step + 1) == entry_ref[step])
        def _():
            copy = pltpu.make_async_copy(noise_ref.at[step], out_ref, sem)
            copy.start()
            copy.wait()

    return pl.pallas_call(
        kernel,
        out_shape=jax.ShapeDtypeStruct(state.shape, BF16),
        in_specs=[SMEM, SMEM, SMEM, VMEM, VMEM, VMEM, HBM],
        out_specs=VMEM,
        scratch_shapes=[pltpu.SemaphoreType.DMA(())],
        compiler_params=params(8),
    )(levels, entry, step_size, state, kept, received, *in_hbm(fresh_noise))


def on_device(
    latents, fresh_noise, levels, pattern, entry, level_scale, level_shift, step_size, qk_gain, wq, wk, wv, wo
):
    count = lax.axis_size("queue")
    mine = latents[0]
    other = swap_cores(mine)
    rows, wk, wv = prepare(levels, level_scale, level_shift, wk, wv)
    for step in range(ITERS):
        if step == 0:
            whole, own = first_keys_values(mine, other, rows, qk_gain, wk, wv)
        else:
            state, whole, own = next_keys_values(
                step, mine, other, terms, received, rows, qk_gain, wk, wv, levels, entry, step_size
            )
        links = [i for i in range(count) if (i + step) % count != count - 1]
        before = lax.ppermute(own, "queue", [(i, (i + 1) % count) for i in links])
        after = lax.ppermute(own, "queue", [((i + 1) % count, i) for i in links])
        query, bias = queries(step, whole, qk_gain, wq, pattern)
        terms = attend_project(step, query, bias, before, own, after, wo, fresh_noise, entry)
        if step < ITERS - 1:
            received = [swap_cores(term) for term in terms]
    state = last_update(state, terms[0], swap_cores(terms[1]), fresh_noise, levels, entry, step_size)
    route = [(i, (i + ITERS) % count) for i in range(count)]
    return lax.ppermute(state, "queue", route)[None]


def solution(mesh):
    return jax.shard_map(
        on_device,
        mesh=mesh,
        in_specs=(
            P("queue", "seq", None),
            P(None, "seq", None),
            P(),
            P(),
            P(),
            P(),
            P(),
            P(),
            P(),
            P(None, "seq"),
            P(None, "seq"),
            P(None, "seq"),
            P("seq", None),
        ),
        out_specs=P("queue", "seq", None),
        check_vma=False,
    )
```

```python
import math

import jax
import jax.numpy as jnp
from jax import lax
from jax.experimental import pallas as pl
from jax.experimental.pallas import tpu as pltpu
from jax.sharding import PartitionSpec as P

HD = 64
FRAMES = 4
ITERS = 2
LANES = 128
EPS = 1e-06
CLOSED = -30000.0
BLOCK = 256
OUT_BLOCK = 768
UNITS = 3
CHUNKS = ((0, 1), (2,))
LAST_COLUMNS = 2
MIB = 1 << 20
F32 = jnp.float32
BF16 = jnp.bfloat16

SMEM = pl.BlockSpec(memory_space=pltpu.SMEM)
VMEM = pl.BlockSpec(memory_space=pltpu.VMEM)
HBM = pl.BlockSpec(memory_space=pltpu.HBM)


def swap_cores(block):
    return lax.ppermute(block, "seq", [(0, 1), (1, 0)])


def in_hbm(*arrays):
    return tuple(pltpu.with_memory_space_constraint(array, pltpu.HBM) for array in arrays)


def params(mib):
    return pltpu.CompilerParams(vmem_limit_bytes=mib * MIB)


def slot_of(step):
    return lax.rem(lax.axis_index("queue") + step, lax.axis_size("queue"))


def modulated_rows(values, scale_row, shift_row):
    normed = values * lax.rsqrt(jnp.mean(values * values, axis=-1, keepdims=True) + EPS)
    return (normed * scale_row + shift_row).astype(BF16)


def head_normed(values, gain_row):
    width = values.shape[1]
    squares = values * values
    high = squares.astype(BF16)
    low = (squares - high.astype(F32)).astype(BF16)
    row = lax.broadcasted_iota(jnp.int32, (width, width), 0)
    column = lax.broadcasted_iota(jnp.int32, (width, width), 1)
    same = (row // HD == column // HD).astype(BF16)
    sums = jnp.dot(high, same, preferred_element_type=F32) + jnp.dot(low, same, preferred_element_type=F32)
    return values * lax.rsqrt(sums * (1.0 / HD) + EPS) * gain_row


def window_bias(pattern_ref, bias_ref, slot, frame_rows):
    count, core = lax.axis_size("queue"), lax.axis_index("seq")
    odd = lax.rem(lax.axis_index("queue"), 2)
    lane = lax.broadcasted_iota(jnp.int32, (1, LANES), 1)
    half = FRAMES // 2
    for i, block in enumerate((1, 2 - 2 * odd, 2 * odd)):
        absent = slot == jnp.where(block == 0, 0, count - 1)
        for at in range(FRAMES):
            key_frame = lax.rem(at + half * core, FRAMES)
            row = jnp.zeros((1, LANES), F32)
            for f in range(FRAMES):
                if i == 0 and f == at:
                    continue
                closed = pattern_ref[lax.rem(f + half * core, FRAMES), block * FRAMES + key_frame] != 1
                if i > 0:
                    closed = jnp.logical_or(closed, absent)
                row = row + jnp.where(lane == f, jnp.where(closed, CLOSED, 0.0), 0.0)
            first = at * frame_rows
            bias_ref[i, first : first + frame_rows, :] = jnp.broadcast_to(row, (frame_rows, LANES)).astype(BF16)


def weight_copies(wk_ref, wv_ref, chunk, out_ref, sems):
    width = out_ref.shape[2]
    columns = pl.ds(chunk * width, width)
    return [
        pltpu.make_async_copy(ref.at[:, columns], out_ref.at[i], sems.at[i]) for i, ref in enumerate((wk_ref, wv_ref))
    ]


def weight_shape(wk):
    return jax.ShapeDtypeStruct((2, wk.shape[0], wk.shape[1] // UNITS), BF16)


def prepare(levels, level_scale, level_shift, wk, wv):
    depth = level_scale.shape[1]

    def kernel(levels_ref, scale_ref, shift_ref, wk_ref, wv_ref, rows_ref, weights_ref, held, levels_sm, sems, weight_sems):
        first = pltpu.make_async_copy(levels_ref, levels_sm, sems.at[0])
        first.start()
        tables = [
            pltpu.make_async_copy(scale_ref, held.at[0], sems.at[1]),
            pltpu.make_async_copy(shift_ref, held.at[1], sems.at[2]),
        ]
        weights = weight_copies(wk_ref, wv_ref, 0, weights_ref, weight_sems)
        for copy in tables + weights:
            copy.start()
        for copy in [first] + tables:
            copy.wait()
        for step in range(ITERS):
            row = pl.ds(levels_sm[slot_of(step)], 1)
            rows_ref[step, 0:1, :] = 1.0 + held[0, row, :]
            rows_ref[step, 1:2, :] = held[1, row, :]
        for copy in weights:
            copy.wait()

    return pl.pallas_call(
        kernel,
        out_shape=(jax.ShapeDtypeStruct((ITERS, 2, depth), F32), weight_shape(wk)),
        in_specs=[HBM] * 5,
        out_specs=(VMEM, VMEM),
        scratch_shapes=[
            pltpu.VMEM((2, *level_scale.shape), F32),
            pltpu.SMEM(levels.shape, jnp.int32),
            pltpu.SemaphoreType.DMA((3,)),
            pltpu.SemaphoreType.DMA((2,)),
        ],
        compiler_params=params(8),
    )(*in_hbm(levels, level_scale, level_shift, wk, wv))


def project(whole, gain_ref, weights_refs, out_ref):
    for i, weights_ref in enumerate(weights_refs):
        width = weights_ref.shape[2]
        columns = slice(i * width, (i + 1) * width)
        keys = jnp.dot(whole[...], weights_ref[0], preferred_element_type=F32)
        gain = jnp.concatenate([gain_ref[1:2, :]] * (width // HD), axis=1)
        out_ref[0, :, columns] = head_normed(keys, gain).astype(BF16)
        out_ref[1, :, columns] = jnp.dot(whole[...], weights_ref[1], preferred_element_type=F32).astype(BF16)


def first_modulated(mine, other, rows, qk_gain, weights, wk, wv):
    half, depth = mine.shape
    unit = weights.shape[2]
    chunk = CHUNKS[0]

    def kernel(mine_ref, other_ref, rows_ref, gain_ref, weights_ref, wk_ref, wv_ref, whole, out_ref, *rest):
        more, sems = rest[: UNITS - 1], rest[-1]
        copies = [weight_copies(wk_ref, wv_ref, i + 1, ref, sems.at[i]) for i, ref in enumerate(more)]
        for pair in copies:
            for copy in pair:
                copy.start()
        scale_row, shift_row = rows_ref[0, 0:1, :], rows_ref[0, 1:2, :]
        whole[:half, :] = modulated_rows(mine_ref[...].astype(F32), scale_row, shift_row)
        whole[half:, :] = modulated_rows(other_ref[...].astype(F32), scale_row, shift_row)
        project(whole, gain_ref, [weights_ref], out_ref.at[:, :, pl.ds(0, unit)])
        for i, pair in enumerate(copies):
            for copy in pair:
                copy.wait()
            if i + 1 in chunk:
                project(whole, gain_ref, [more[i]], out_ref.at[:, :, pl.ds((i + 1) * unit, unit)])

    return pl.pallas_call(
        kernel,
        out_shape=(
            jax.ShapeDtypeStruct((2 * half, depth), BF16),
            jax.ShapeDtypeStruct((2, 2 * half, unit * len(chunk)), BF16),
            *[weight_shape(wk)] * (UNITS - 1),
        ),
        in_specs=[VMEM] * 5 + [HBM] * 2,
        out_specs=(VMEM,) * (UNITS + 1),
        scratch_shapes=[pltpu.SemaphoreType.DMA((UNITS - 1, 2))],
        compiler_params=params(8),
    )(mine, other, rows, qk_gain, weights, *in_hbm(wk, wv))


def next_modulated(step, mine, other, terms, received, rows, qk_gain, weights, levels, entry, step_size):
    half, depth = mine.shape
    unit = weights[0].shape[2]
    chunk = CHUNKS[0]

    def kernel(levels_ref, entry_ref, size_ref, mine_ref, other_ref, term_mine, term_other, their_own, their_mine, rows_ref, gain_ref, *rest):
        weights_refs, (state_ref, whole, out_ref) = rest[:-3], rest[-3:]
        slot = slot_of(step - 1)
        fresh = slot_of(step) == entry_ref[step - 1]
        size = size_ref[levels_ref[slot]]
        scale_row, shift_row = rows_ref[step, 0:1, :], rows_ref[step, 1:2, :]

        def moved(state, term_a, term_b, noise):
            velocity = term_a[...].astype(F32) + term_b[...].astype(F32)
            updated = (state[...].astype(F32) + size * velocity).astype(BF16)
            return jnp.where(fresh, noise[...], updated)

        new = moved(mine_ref, term_mine, their_mine, term_mine)
        state_ref[...] = new
        whole[:half, :] = modulated_rows(new.astype(F32), scale_row, shift_row)
        new = moved(other_ref, term_other, their_own, their_own)
        whole[half:, :] = modulated_rows(new.astype(F32), scale_row, shift_row)
        project(whole, gain_ref, weights_refs, out_ref)

    return pl.pallas_call(
        kernel,
        out_shape=(
            jax.ShapeDtypeStruct((half, depth), BF16),
            jax.ShapeDtypeStruct((2 * half, depth), BF16),
            jax.ShapeDtypeStruct((2, 2 * half, unit * len(chunk)), BF16),
        ),
        in_specs=[SMEM] * 3 + [VMEM] * (8 + len(chunk)),
        out_specs=(VMEM,) * 3,
        compiler_params=params(8),
    )(levels, entry, step_size, mine, other, *terms, *received, rows, qk_gain, *[weights[i] for i in chunk])


def keys_values(whole, qk_gain, weights):
    def kernel(whole_ref, gain_ref, *rest):
        project(whole_ref, gain_ref, rest[:-1], rest[-1])

    width = sum(block.shape[2] for block in weights)
    return pl.pallas_call(
        kernel,
        out_shape=jax.ShapeDtypeStruct((2, whole.shape[0], width), BF16),
        in_specs=[VMEM] * (2 + len(weights)),
        out_specs=VMEM,
        compiler_params=params(8),
    )(whole, qk_gain, *weights)


def attention_parts(query_pair, blocks):
    tokens = query_pair.shape[0]
    lane = lax.broadcasted_iota(jnp.int32, (tokens, LANES), 1)
    frame = lax.broadcasted_iota(jnp.int32, (tokens, LANES), 0) // (tokens // FRAMES)
    frame_of = (lane == frame).astype(BF16)
    first = lane < HD
    ones = jnp.ones((tokens, LANES), BF16)
    parts = []
    for which in (first, jnp.logical_not(first)):
        one = jnp.concatenate([jnp.where(which, query_pair, jnp.zeros_like(query_pair)), frame_of], axis=1)
        both = None
        for keys, values, bias in blocks:
            scores = lax.dot_general(
                one, jnp.concatenate([keys, bias], axis=1), (((1,), (1,)), ((), ())), preferred_element_type=F32
            )
            weights = jnp.exp2(scores).astype(BF16)
            part = jnp.dot(weights, jnp.concatenate([values, ones], axis=1), preferred_element_type=F32)
            both = part if both is None else both + part
        parts.append(both)
    return (
        jnp.where(first, parts[0][:, :LANES], parts[1][:, :LANES]),
        jnp.where(first, parts[0][:, LANES:], parts[1][:, LANES:]),
    )


def queries(step, whole, qk_gain, wq, pattern, own):
    tokens = whole.shape[0]
    width = wq.shape[1]
    scale = math.log2(math.e) / math.sqrt(HD)

    def kernel(pattern_ref, gain_ref, whole_ref, wq_ref, *rest):
        own_refs, (out_ref, bias_ref, sums_ref) = rest[:-3], rest[-3:]
        window_bias(pattern_ref, bias_ref, slot_of(step), tokens // FRAMES)
        gain = jnp.concatenate([gain_ref[0:1, :] * scale] * (BLOCK // HD), axis=1)
        for block in range(width // BLOCK):
            columns = slice(block * BLOCK, (block + 1) * BLOCK)
            query = jnp.dot(whole_ref[...], wq_ref[:, columns], preferred_element_type=F32)
            out_ref[:, columns] = head_normed(query, gain).astype(BF16)
        start = 0
        for ref in own_refs:
            for first in range(0, ref.shape[2], LANES):
                at = slice(first, first + LANES)
                columns = slice(start, start + LANES)
                start += LANES
                top, bottom = attention_parts(out_ref[:, columns], [(ref[0, :, at], ref[1, :, at], bias_ref[0])])
                sums_ref[0, :, columns] = top
                sums_ref[1, :, columns] = bottom

    return pl.pallas_call(
        kernel,
        out_shape=(
            jax.ShapeDtypeStruct((tokens, width), BF16),
            jax.ShapeDtypeStruct((3, tokens, LANES), BF16),
            jax.ShapeDtypeStruct((2, tokens, width), F32),
        ),
        in_specs=[SMEM] + [VMEM] * (3 + len(own)),
        out_specs=(VMEM,) * 3,
        compiler_params=params(8),
    )(pattern, qk_gain, whole, wq, *own)


def attend_columns(start, query_ref, bias_ref, sums_ref, partner_ref, neighbour_ref, attended):
    for first in range(0, partner_ref.shape[2], LANES):
        at = slice(first, first + LANES)
        columns = slice(start + first, start + first + LANES)
        blocks = [(ref[0, :, at], ref[1, :, at], bias_ref[i + 1]) for i, ref in enumerate((partner_ref, neighbour_ref))]
        top, bottom = attention_parts(query_ref[:, columns], blocks)
        top = top + sums_ref[0, :, columns]
        bottom = bottom + sums_ref[1, :, columns]
        attended[:, columns] = (top / bottom).astype(BF16)


def attend(query, bias, sums, partner, neighbour):
    def kernel(*refs):
        attend_columns(0, *refs)

    return pl.pallas_call(
        kernel,
        out_shape=jax.ShapeDtypeStruct(query.shape, BF16),
        in_specs=[VMEM] * 5,
        out_specs=VMEM,
        compiler_params=params(8),
    )(query, bias, sums, partner, neighbour)


def project_term(attended, wo_ref, first, keep_ref, send_ref):
    half = keep_ref.shape[0]
    for start in range(0, keep_ref.shape[1], OUT_BLOCK):
        columns = slice(start, start + OUT_BLOCK)
        term = jnp.dot(
            attended[...], wo_ref[:, first + start : first + start + OUT_BLOCK], preferred_element_type=F32
        ).astype(BF16)
        keep_ref[:, columns] = term[:half]
        send_ref[:, columns] = term[half:]


def attend_project(step, query, bias, sums, partner, neighbour, so_far, wo, fresh_noise, entry, width):
    tokens = query.shape[0]
    half = tokens // 2
    start = query.shape[1] - partner.shape[2]

    def kernel(entry_ref, query_ref, bias_ref, sums_ref, partner_ref, neighbour_ref, so_far_ref, wo_ref, noise_ref, keep_ref, send_ref, attended, sem):
        attended[:, :start] = so_far_ref[:, :start]
        attend_columns(start, query_ref, bias_ref, sums_ref, partner_ref, neighbour_ref, attended)
        project_term(attended, wo_ref, 0, keep_ref, send_ref)
        if step < ITERS - 1:

            @pl.when(slot_of(step + 1) == entry_ref[step])
            def _():
                copy = pltpu.make_async_copy(noise_ref.at[step], keep_ref, sem)
                copy.start()
                copy.wait()

    out = jax.ShapeDtypeStruct((half, width), BF16)
    return pl.pallas_call(
        kernel,
        out_shape=(out, out, jax.ShapeDtypeStruct(query.shape, BF16)),
        in_specs=[SMEM] + [VMEM] * 7 + [HBM],
        out_specs=(VMEM,) * 3,
        scratch_shapes=[pltpu.SemaphoreType.DMA(())],
        compiler_params=params(8),
    )(entry, query, bias, sums, partner, neighbour, so_far, wo, *in_hbm(fresh_noise))


def more_term(attended, wo, first, width):
    def kernel(attended_ref, wo_ref, keep_ref, send_ref):
        project_term(attended_ref, wo_ref, first, keep_ref, send_ref)

    out = jax.ShapeDtypeStruct((attended.shape[0] // 2, width), BF16)
    return pl.pallas_call(
        kernel,
        out_shape=(out, out),
        in_specs=[VMEM, VMEM],
        out_specs=(VMEM, VMEM),
        compiler_params=params(8),
    )(attended, wo)


def last_update(state, first, kept, received, fresh_noise, levels, entry, step_size):
    step = ITERS - 1
    width = kept.shape[1]

    def kernel(levels_ref, entry_ref, size_ref, state_ref, kept_ref, received_ref, noise_ref, out_ref, sem):
        velocity = kept_ref[...].astype(F32) + received_ref[...].astype(F32)
        size = size_ref[levels_ref[slot_of(step)]]
        out_ref[...] = (state_ref[:, first : first + width].astype(F32) + size * velocity).astype(BF16)

        @pl.when(slot_of(step + 1) == entry_ref[step])
        def _():
            copy = pltpu.make_async_copy(noise_ref.at[step, :, pl.ds(first, width)], out_ref, sem)
            copy.start()
            copy.wait()

    return pl.pallas_call(
        kernel,
        out_shape=jax.ShapeDtypeStruct(kept.shape, BF16),
        in_specs=[SMEM, SMEM, SMEM, VMEM, VMEM, VMEM, HBM],
        out_specs=VMEM,
        scratch_shapes=[pltpu.SemaphoreType.DMA(())],
        compiler_params=params(8),
    )(levels, entry, step_size, state, kept, received, *in_hbm(fresh_noise))


def exchanged(step, block):
    count = lax.axis_size("queue")
    got = []
    for first in (1, 0):
        pairs = []
        for i in range(first, count, 2):
            if (i + step) % count != count - 1:
                pairs += [(i, (i + 1) % count), ((i + 1) % count, i)]
        got.append(lax.ppermute(block, "queue", pairs))
    return got[::-1]


def on_device(
    latents, fresh_noise, levels, pattern, entry, level_scale, level_shift, step_size, qk_gain, wq, wk, wv, wo
):
    count = lax.axis_size("queue")
    mine = latents[0]
    depth = mine.shape[1]
    other = swap_cores(mine)
    rows, *weights = prepare(levels, level_scale, level_shift, wk, wv)
    for step in range(ITERS):
        if step == 0:
            whole, own, *more = first_modulated(mine, other, rows, qk_gain, weights[0], wk, wv)
            weights += more
        else:
            state, whole, own = next_modulated(
                step, mine, other, terms, received, rows, qk_gain, weights, levels, entry, step_size
            )
        theirs = exchanged(step, own)
        late = keys_values(whole, qk_gain, [weights[i] for i in CHUNKS[1]])
        late_theirs = exchanged(step, late)
        query, bias, sums = queries(step, whole, qk_gain, wq, pattern, [own, late])
        attended = attend(query, bias, sums, *theirs)
        width = depth if step < ITERS - 1 else depth // LAST_COLUMNS
        *terms, attended = attend_project(
            step, query, bias, sums, *late_theirs, attended, wo, fresh_noise, entry, width
        )
        if step < ITERS - 1:
            received = [swap_cores(term) for term in terms]
    route = [(i, (i + ITERS) % count) for i in range(count)]
    result = []
    for first in range(0, depth, width):
        if first > 0:
            terms = more_term(attended, wo, first, width)
        part = last_update(state, first, terms[0], swap_cores(terms[1]), fresh_noise, levels, entry, step_size)
        result.append(lax.ppermute(part, "queue", route))
    return jnp.concatenate(result, axis=1)[None]


def solution(mesh):
    return jax.shard_map(
        on_device,
        mesh=mesh,
        in_specs=(
            P("queue", "seq", None),
            P(None, "seq", None),
            P(),
            P(),
            P(),
            P(),
            P(),
            P(),
            P(),
            P(None, "seq"),
            P(None, "seq"),
            P(None, "seq"),
            P("seq", None),
        ),
        out_specs=P("queue", "seq", None),
        check_vma=False,
    )
```

```python
import math

import jax
import jax.numpy as jnp
from jax import lax
from jax.experimental import pallas as pl
from jax.experimental.pallas import tpu as pltpu
from jax.sharding import PartitionSpec as P

HD = 64
FRAMES = 4
ITERS = 2
LANES = 128
EPS = 1e-06
CLOSED = -30000.0
BLOCK = 256
OUT_BLOCK = 768
LAST_COLUMNS = 2
MIB = 1 << 20
F32 = jnp.float32
BF16 = jnp.bfloat16

SMEM = pl.BlockSpec(memory_space=pltpu.SMEM)
VMEM = pl.BlockSpec(memory_space=pltpu.VMEM)
HBM = pl.BlockSpec(memory_space=pltpu.HBM)


def swap_cores(block):
    return lax.ppermute(block, "seq", [(0, 1), (1, 0)])


def in_hbm(*arrays):
    return tuple(pltpu.with_memory_space_constraint(array, pltpu.HBM) for array in arrays)


def params(mib):
    return pltpu.CompilerParams(vmem_limit_bytes=mib * MIB)


def slot_of(step):
    return lax.rem(lax.axis_index("queue") + step, lax.axis_size("queue"))


def modulated_rows(values, scale_row, shift_row):
    normed = values * lax.rsqrt(jnp.mean(values * values, axis=-1, keepdims=True) + EPS)
    return (normed * scale_row + shift_row).astype(BF16)


def head_normed(values, gain_row):
    rows, width = values.shape
    blocks = [values[:, first : first + BLOCK] for first in range(0, width, BLOCK)]
    stacked = jnp.concatenate(blocks, axis=0)
    row = lax.broadcasted_iota(jnp.int32, (BLOCK, BLOCK), 0)
    column = lax.broadcasted_iota(jnp.int32, (BLOCK, BLOCK), 1)
    same = (row // HD == column // HD).astype(BF16)
    sums = jnp.dot((stacked * stacked).astype(BF16), same, preferred_element_type=F32)
    normed = (stacked * lax.rsqrt(sums * (1.0 / HD) + EPS) * gain_row).astype(BF16)
    return jnp.concatenate([normed[i * rows : (i + 1) * rows] for i in range(len(blocks))], axis=1)


def gain_columns(gain_ref, which):
    return jnp.concatenate([gain_ref[which : which + 1, :]] * (BLOCK // HD), axis=1)


def window_bias(pattern_ref, bias_ref, slot, frame_rows):
    count, core = lax.axis_size("queue"), lax.axis_index("seq")
    odd = lax.rem(lax.axis_index("queue"), 2)
    lane = lax.broadcasted_iota(jnp.int32, (1, LANES), 1)
    half = FRAMES // 2
    for i, block in enumerate((1, 2 - 2 * odd, 2 * odd)):
        absent = slot == jnp.where(block == 0, 0, count - 1)
        for at in range(FRAMES):
            key_frame = lax.rem(at + half * core, FRAMES)
            row = jnp.zeros((1, LANES), F32)
            for f in range(FRAMES):
                if i == 0 and f == at:
                    continue
                closed = pattern_ref[lax.rem(f + half * core, FRAMES), block * FRAMES + key_frame] != 1
                if i > 0:
                    closed = jnp.logical_or(closed, absent)
                row = row + jnp.where(lane == f, jnp.where(closed, CLOSED, 0.0), 0.0)
            to, first = (0, at) if i == 0 else (1 + at // half, (i - 1) * half + at % half)
            rows = slice(first * frame_rows, (first + 1) * frame_rows)
            bias_ref[to, rows, :] = jnp.broadcast_to(row, (frame_rows, LANES)).astype(BF16)


def project(modulated, gain_ref, wk_ref, wv_ref, out_ref):
    keys = jnp.dot(modulated, wk_ref[...], preferred_element_type=F32)
    out_ref[0] = head_normed(keys, gain_columns(gain_ref, 1))
    out_ref[1] = jnp.dot(modulated, wv_ref[...], preferred_element_type=F32).astype(BF16)


def first_half(state, levels, level_scale, level_shift, qk_gain, wk, wv):
    half, depth = state.shape
    width = wk.shape[1]

    def kernel(levels_ref, scale_ref, shift_ref, state_hbm, gain_hbm, wk_ref, wv_ref, modulated_ref, out_ref, rows_ref, wk_out, wv_out, held, state_ref, gain_ref, levels_sm, sems, weight_sems):
        first = pltpu.make_async_copy(levels_ref, levels_sm, sems.at[0])
        first.start()
        tables = [
            pltpu.make_async_copy(scale_ref, held.at[0], sems.at[1]),
            pltpu.make_async_copy(shift_ref, held.at[1], sems.at[2]),
            pltpu.make_async_copy(state_hbm, state_ref, sems.at[3]),
            pltpu.make_async_copy(gain_hbm, gain_ref, sems.at[4]),
        ]
        parts = [pl.ds(0, depth // 2), pl.ds(depth // 2, depth // 2)]
        weights = [
            pltpu.make_async_copy(ref.at[part], out.at[part], weight_sems.at[2 * i + j])
            for i, (ref, out) in enumerate(((wk_ref, wk_out), (wv_ref, wv_out)))
            for j, part in enumerate(parts)
        ]
        for copy in tables + weights[:2]:
            copy.start()
        for copy in [first] + tables:
            copy.wait()
        for step in range(ITERS):
            row = pl.ds(levels_sm[slot_of(step)], 1)
            rows_ref[step, 0:1, :] = 1.0 + held[0, row, :]
            rows_ref[step, 1:2, :] = held[1, row, :]
        modulated_ref[...] = modulated_rows(state_ref[...].astype(F32), rows_ref[0, 0:1, :], rows_ref[0, 1:2, :])
        for i, weight in enumerate((wk_out, wv_out)):
            total = None
            for j, part in enumerate(parts):
                weights[2 * i + j].wait()
                if i == 0:
                    weights[2 + j].start()
                product = jnp.dot(modulated_ref[:, part], weight[part, :], preferred_element_type=F32)
                total = product if total is None else total + product
            out_ref[i] = head_normed(total, gain_columns(gain_ref, 1)) if i == 0 else total.astype(BF16)

    return pl.pallas_call(
        kernel,
        out_shape=(
            jax.ShapeDtypeStruct((half, depth), BF16),
            jax.ShapeDtypeStruct((2, half, width), BF16),
            jax.ShapeDtypeStruct((ITERS, 2, depth), F32),
            jax.ShapeDtypeStruct(wk.shape, BF16),
            jax.ShapeDtypeStruct(wv.shape, BF16),
        ),
        in_specs=[HBM] * 7,
        out_specs=(VMEM,) * 5,
        scratch_shapes=[
            pltpu.VMEM((2, *level_scale.shape), F32),
            pltpu.VMEM(state.shape, BF16),
            pltpu.VMEM(qk_gain.shape, F32),
            pltpu.SMEM(levels.shape, jnp.int32),
            pltpu.SemaphoreType.DMA((5,)),
            pltpu.SemaphoreType.DMA((4,)),
        ],
        compiler_params=params(8),
    )(*in_hbm(levels, level_scale, level_shift, state, qk_gain, wk, wv))


def next_half(step, state, kept, received, fresh_noise, rows, qk_gain, wk, wv, levels, entry, step_size):
    half, depth = state.shape
    width = wk.shape[1]

    def kernel(levels_ref, entry_ref, size_ref, state_ref, kept_ref, received_ref, rows_ref, gain_ref, wk_ref, wv_ref, noise_ref, new_ref, modulated_ref, out_ref, sem):
        size = size_ref[levels_ref[slot_of(step - 1)]]
        velocity = kept_ref[...].astype(F32) + received_ref[...].astype(F32)
        new_ref[...] = (state_ref[...].astype(F32) + size * velocity).astype(BF16)

        @pl.when(slot_of(step) == entry_ref[step - 1])
        def _():
            copy = pltpu.make_async_copy(noise_ref.at[step - 1], new_ref, sem)
            copy.start()
            copy.wait()

        modulated_ref[...] = modulated_rows(new_ref[...].astype(F32), rows_ref[step, 0:1, :], rows_ref[step, 1:2, :])
        project(modulated_ref[...], gain_ref, wk_ref, wv_ref, out_ref)

    return pl.pallas_call(
        kernel,
        out_shape=(
            jax.ShapeDtypeStruct((half, depth), BF16),
            jax.ShapeDtypeStruct((half, depth), BF16),
            jax.ShapeDtypeStruct((2, half, width), BF16),
        ),
        in_specs=[SMEM] * 3 + [VMEM] * 7 + [HBM],
        out_specs=(VMEM,) * 3,
        scratch_shapes=[pltpu.SemaphoreType.DMA(())],
        compiler_params=params(8),
    )(levels, entry, step_size, state, kept, received, rows, qk_gain, wk, wv, *in_hbm(fresh_noise))


def other_half(modulated, qk_gain, wk, wv, wq):
    half = modulated.shape[0]
    width = wk.shape[1]
    load = wq is not None

    def kernel(modulated_ref, gain_ref, wk_ref, wv_ref, *rest):
        out_ref = rest[load]
        if load:
            copy = pltpu.make_async_copy(rest[0], rest[2], rest[3])
            copy.start()
        project(modulated_ref[...], gain_ref, wk_ref, wv_ref, out_ref)
        if load:
            copy.wait()

    out = jax.ShapeDtypeStruct((2, half, width), BF16)
    return pl.pallas_call(
        kernel,
        out_shape=(out, jax.ShapeDtypeStruct(wq.shape, BF16)) if load else (out,),
        in_specs=[VMEM] * 4 + [HBM] * load,
        out_specs=(VMEM,) * (1 + load),
        scratch_shapes=[pltpu.SemaphoreType.DMA(())] * load,
        compiler_params=params(8),
    )(modulated, qk_gain, wk, wv, *(in_hbm(wq) if load else ()))


def attention_parts(query_pair, keys, values, bias):
    tokens = query_pair.shape[0]
    lane = lax.broadcasted_iota(jnp.int32, (tokens, LANES), 1)
    frame = lax.broadcasted_iota(jnp.int32, (tokens, LANES), 0) // (tokens // FRAMES)
    frame_of = (lane == frame).astype(BF16)
    first = lane < HD
    ones = jnp.ones((tokens, LANES), BF16)
    parts = []
    for which in (first, jnp.logical_not(first)):
        one = jnp.concatenate([jnp.where(which, query_pair, jnp.zeros_like(query_pair)), frame_of], axis=1)
        scores = lax.dot_general(
            one, jnp.concatenate([keys, bias], axis=1), (((1,), (1,)), ((), ())), preferred_element_type=F32
        )
        weights = jnp.exp2(scores).astype(BF16)
        parts.append(jnp.dot(weights, jnp.concatenate([values, ones], axis=1), preferred_element_type=F32))
    return (
        jnp.where(first, parts[0][:, :LANES], parts[1][:, :LANES]),
        jnp.where(first, parts[0][:, LANES:], parts[1][:, LANES:]),
    )


def pair_parts(query_ref, first_ref, second_ref, bias, columns):
    keys, values = (
        jnp.concatenate([first_ref[i, :, columns], second_ref[i, :, columns]], axis=0) for i in range(2)
    )
    return attention_parts(query_ref[:, columns], keys, values, bias)


def queries(step, mine, other, qk_gain, wq, pattern, own, own_other, wo):
    half, _ = mine.shape
    tokens, width = 2 * half, wq.shape[1]
    scale = math.log2(math.e) / math.sqrt(HD)
    load = wo is not None

    def kernel(pattern_ref, gain_ref, mine_ref, other_ref, wq_ref, own_ref, own_other_ref, *rest):
        out_ref, bias_ref, sums_ref = rest[load : load + 3]
        whole = rest[-1 - load]
        if load:
            copy = pltpu.make_async_copy(rest[0], rest[load + 3], rest[-1])
            copy.start()
        whole[:half, :] = mine_ref[...]
        whole[half:, :] = other_ref[...]
        window_bias(pattern_ref, bias_ref, slot_of(step), tokens // FRAMES)
        query = jnp.dot(whole[...], wq_ref[...], preferred_element_type=F32)
        out_ref[...] = head_normed(query, gain_columns(gain_ref, 0) * scale)
        for first in range(0, width, LANES):
            columns = slice(first, first + LANES)
            sums_ref[0, :, columns], sums_ref[1, :, columns] = pair_parts(out_ref, own_ref, own_other_ref, bias_ref[0], columns)
        if load:
            copy.wait()

    out_shape = [
        jax.ShapeDtypeStruct((tokens, width), BF16),
        jax.ShapeDtypeStruct((3, tokens, LANES), BF16),
        jax.ShapeDtypeStruct((2, tokens, width), F32),
    ]
    if load:
        out_shape.append(jax.ShapeDtypeStruct(wo.shape, BF16))
    return pl.pallas_call(
        kernel,
        out_shape=out_shape,
        in_specs=[SMEM] + [VMEM] * 6 + [HBM] * load,
        out_specs=[VMEM] * (3 + load),
        scratch_shapes=[pltpu.VMEM((tokens, mine.shape[1]), BF16)] + [pltpu.SemaphoreType.DMA(())] * load,
        compiler_params=params(8),
    )(pattern, qk_gain, mine, other, wq, own, own_other, *(in_hbm(wo) if load else ()))


def attend(query, bias, sums, partner, neighbour):
    def kernel(query_ref, bias_ref, sums_ref, partner_ref, neighbour_ref, out_ref):
        for first in range(0, query_ref.shape[1], LANES):
            columns = slice(first, first + LANES)
            parts = pair_parts(query_ref, partner_ref, neighbour_ref, bias_ref[1], columns)
            for i in range(2):
                out_ref[i, :, columns] = sums_ref[i, :, columns] + parts[i]

    return pl.pallas_call(
        kernel,
        out_shape=jax.ShapeDtypeStruct(sums.shape, F32),
        in_specs=[VMEM] * 5,
        out_specs=VMEM,
        compiler_params=params(8),
    )(query, bias, sums, partner, neighbour)


def project_term(attended, wo_ref, rows, first, outs):
    for start in range(0, outs[0].shape[1], OUT_BLOCK):
        term = jnp.dot(
            attended[rows, :], wo_ref[:, first + start : first + start + OUT_BLOCK], preferred_element_type=F32
        ).astype(BF16)
        height = outs[0].shape[0]
        for i, out_ref in enumerate(outs):
            out_ref[:, start : start + OUT_BLOCK] = term[i * height : (i + 1) * height]


def attend_project(query, bias, sums, partner, neighbour, wo, both, width):
    tokens = query.shape[0]
    half = tokens // 2

    def kernel(query_ref, bias_ref, sums_ref, partner_ref, neighbour_ref, wo_ref, attended, *outs):
        for first in range(0, query_ref.shape[1], LANES):
            columns = slice(first, first + LANES)
            top, bottom = pair_parts(query_ref, partner_ref, neighbour_ref, bias_ref[2], columns)
            top = top + sums_ref[0, :, columns]
            bottom = bottom + sums_ref[1, :, columns]
            attended[:, columns] = (top / bottom).astype(BF16)
        project_term(attended, wo_ref, slice(0 if both else half, tokens), 0, outs)

    out = jax.ShapeDtypeStruct((half, width), BF16)
    return pl.pallas_call(
        kernel,
        out_shape=(jax.ShapeDtypeStruct(query.shape, BF16), *[out] * (1 + both)),
        in_specs=[VMEM] * 6,
        out_specs=(VMEM,) * (2 + both),
        compiler_params=params(8),
    )(query, bias, sums, partner, neighbour, wo)


def more_term(attended, wo, both, first, width):
    tokens = attended.shape[0]
    half = tokens // 2

    def kernel(attended_ref, wo_ref, *outs):
        project_term(attended_ref, wo_ref, slice(0, tokens if both else half), first, outs)

    out = jax.ShapeDtypeStruct((half, width), BF16)
    return pl.pallas_call(
        kernel,
        out_shape=(out,) * (1 + both),
        in_specs=[VMEM, VMEM],
        out_specs=(VMEM,) * (1 + both),
        compiler_params=params(8),
    )(attended, wo)


def last_update(state, first, kept, received, fresh_noise, levels, entry, step_size):
    step = ITERS - 1
    width = kept.shape[1]

    def kernel(levels_ref, entry_ref, size_ref, state_ref, kept_ref, received_ref, noise_ref, out_ref, sem):
        velocity = kept_ref[...].astype(F32) + received_ref[...].astype(F32)
        size = size_ref[levels_ref[slot_of(step)]]
        out_ref[...] = (state_ref[:, first : first + width].astype(F32) + size * velocity).astype(BF16)

        @pl.when(slot_of(step + 1) == entry_ref[step])
        def _():
            copy = pltpu.make_async_copy(noise_ref.at[step, :, pl.ds(first, width)], out_ref, sem)
            copy.start()
            copy.wait()

    return pl.pallas_call(
        kernel,
        out_shape=jax.ShapeDtypeStruct(kept.shape, BF16),
        in_specs=[SMEM, SMEM, SMEM, VMEM, VMEM, VMEM, HBM],
        out_specs=VMEM,
        scratch_shapes=[pltpu.SemaphoreType.DMA(())],
        compiler_params=params(8),
    )(levels, entry, step_size, state, kept, received, *in_hbm(fresh_noise))


def exchanged(step, partner, block):
    count = lax.axis_size("queue")
    pairs = []
    for i in range(0 if partner else 1, count, 2):
        if (i + step) % count != count - 1:
            pairs += [(i, (i + 1) % count), ((i + 1) % count, i)]
    return lax.ppermute(block, "queue", pairs)


def on_device(
    latents, fresh_noise, levels, pattern, entry, level_scale, level_shift, step_size, qk_gain, wq, wk, wv, wo
):
    count = lax.axis_size("queue")
    state = latents[0]
    depth = state.shape[1]
    for step in range(ITERS):
        if step == 0:
            mine, own, rows, wk, wv = first_half(state, levels, level_scale, level_shift, qk_gain, wk, wv)
        else:
            state, mine, own = next_half(
                step, state, kept, received, fresh_noise, rows, qk_gain, wk, wv, levels, entry, step_size
            )
        other = swap_cores(mine)
        neighbour = exchanged(step, False, own)
        other, own = lax.optimization_barrier((other, own))
        theirs = exchanged(step, True, own), neighbour
        own_other, *loaded = other_half(other, qk_gain, wk, wv, wq if step == 0 else None)
        if loaded:
            wq = loaded[0]
        theirs_other = exchanged(step, True, own_other), exchanged(step, False, own_other)
        query, bias, sums, *loaded = queries(
            step, mine, other, qk_gain, wq, pattern, own, own_other, wo if step == 0 else None
        )
        if loaded:
            wo = loaded[0]
        sums = attend(query, bias, sums, *theirs)
        if step < ITERS - 1:
            attended, sent = attend_project(query, bias, sums, *theirs_other, wo, False, depth)
            received = swap_cores(sent)
            (kept,) = more_term(attended, wo, False, 0, depth)
    width = depth // LAST_COLUMNS
    attended, *terms = attend_project(query, bias, sums, *theirs_other, wo, True, width)
    route = [(i, (i + ITERS) % count) for i in range(count)]
    result = []
    for first in range(0, depth, width):
        if first > 0:
            terms = more_term(attended, wo, True, first, width)
        part = last_update(state, first, terms[0], swap_cores(terms[1]), fresh_noise, levels, entry, step_size)
        result.append(lax.ppermute(part, "queue", route))
    return jnp.concatenate(result, axis=1)[None]


def solution(mesh):
    return jax.shard_map(
        on_device,
        mesh=mesh,
        in_specs=(
            P("queue", "seq", None),
            P(None, "seq", None),
            P(),
            P(),
            P(),
            P(),
            P(),
            P(),
            P(),
            P(None, "seq"),
            P(None, "seq"),
            P(None, "seq"),
            P("seq", None),
        ),
        out_specs=P("queue", "seq", None),
        check_vma=False,
    )
```

```python
import math

import jax
import jax.numpy as jnp
from jax import lax
from jax.experimental import pallas as pl
from jax.experimental.pallas import tpu as pltpu
from jax.sharding import PartitionSpec as P

HD = 64
FRAMES = 4
ITERS = 2
LANES = 128
EPS = 1e-06
CLOSED = -30000.0
BLOCK = 256
OUT_BLOCK = 768
LAST_COLUMNS = 2
MIB = 1 << 20
F32 = jnp.float32
BF16 = jnp.bfloat16

SMEM = pl.BlockSpec(memory_space=pltpu.SMEM)
VMEM = pl.BlockSpec(memory_space=pltpu.VMEM)
HBM = pl.BlockSpec(memory_space=pltpu.HBM)


def swap_cores(block):
    return lax.ppermute(block, "seq", [(0, 1), (1, 0)])


def in_hbm(*arrays):
    return tuple(pltpu.with_memory_space_constraint(array, pltpu.HBM) for array in arrays)


def params(mib):
    return pltpu.CompilerParams(vmem_limit_bytes=mib * MIB)


def slot_of(step):
    return lax.rem(lax.axis_index("queue") + step, lax.axis_size("queue"))


def modulated_rows(values, scale_row, shift_row):
    normed = values * lax.rsqrt(jnp.mean(values * values, axis=-1, keepdims=True) + EPS)
    return (normed * scale_row + shift_row).astype(BF16)


def head_normed(values, gain_row):
    rows, width = values.shape
    blocks = [values[:, first : first + BLOCK] for first in range(0, width, BLOCK)]
    stacked = jnp.concatenate(blocks, axis=0)
    row = lax.broadcasted_iota(jnp.int32, (BLOCK, BLOCK), 0)
    column = lax.broadcasted_iota(jnp.int32, (BLOCK, BLOCK), 1)
    same = (row // HD == column // HD).astype(BF16)
    sums = jnp.dot((stacked * stacked).astype(BF16), same, preferred_element_type=F32)
    normed = (stacked * lax.rsqrt(sums * (1.0 / HD) + EPS) * gain_row).astype(BF16)
    return jnp.concatenate([normed[i * rows : (i + 1) * rows] for i in range(len(blocks))], axis=1)


def gain_columns(gain_ref, which):
    return jnp.concatenate([gain_ref[which : which + 1, :]] * (BLOCK // HD), axis=1)


def window_bias(pattern_ref, bias_ref, slot, frame_rows):
    count, core = lax.axis_size("queue"), lax.axis_index("seq")
    odd = lax.rem(lax.axis_index("queue"), 2)
    lane = lax.broadcasted_iota(jnp.int32, (1, LANES), 1)
    half = FRAMES // 2
    for i, block in enumerate((1, 2 - 2 * odd, 2 * odd)):
        absent = slot == jnp.where(block == 0, 0, count - 1)
        for at in range(FRAMES):
            key_frame = lax.rem(at + half * core, FRAMES)
            row = jnp.zeros((1, LANES), F32)
            for f in range(FRAMES):
                if i == 0 and f == at:
                    continue
                closed = pattern_ref[lax.rem(f + half * core, FRAMES), block * FRAMES + key_frame] != 1
                if i > 0:
                    closed = jnp.logical_or(closed, absent)
                row = row + jnp.where(lane == f, jnp.where(closed, CLOSED, 0.0), 0.0)
            to, first = (0, at) if i == 0 else (1 + at // half, (i - 1) * half + at % half)
            rows = slice(first * frame_rows, (first + 1) * frame_rows)
            bias_ref[to, rows, :] = jnp.broadcast_to(row, (frame_rows, LANES)).astype(BF16)


def project(modulated, gain_ref, wk_ref, wv_ref, out_ref):
    keys = jnp.dot(modulated, wk_ref[...], preferred_element_type=F32)
    out_ref[0] = head_normed(keys, gain_columns(gain_ref, 1))
    out_ref[1] = jnp.dot(modulated, wv_ref[...], preferred_element_type=F32).astype(BF16)


def first_half(state, levels, level_scale, level_shift, qk_gain, wk, wv):
    half, depth = state.shape
    width = wk.shape[1]

    def kernel(levels_ref, scale_ref, shift_ref, state_hbm, gain_hbm, wk_ref, wv_ref, modulated_ref, out_ref, rows_ref, wk_out, wv_out, held, state_ref, gain_ref, levels_sm, sems, weight_sems):
        first = pltpu.make_async_copy(levels_ref, levels_sm, sems.at[0])
        first.start()
        tables = [
            pltpu.make_async_copy(scale_ref, held.at[0], sems.at[1]),
            pltpu.make_async_copy(shift_ref, held.at[1], sems.at[2]),
            pltpu.make_async_copy(state_hbm, state_ref, sems.at[3]),
            pltpu.make_async_copy(gain_hbm, gain_ref, sems.at[4]),
        ]
        parts = [pl.ds(0, depth // 2), pl.ds(depth // 2, depth // 2)]
        weights = [
            pltpu.make_async_copy(ref.at[part], out.at[part], weight_sems.at[2 * i + j])
            for i, (ref, out) in enumerate(((wk_ref, wk_out), (wv_ref, wv_out)))
            for j, part in enumerate(parts)
        ]
        for copy in tables + weights[:3]:
            copy.start()
        for copy in [first] + tables:
            copy.wait()
        for step in range(ITERS):
            row = pl.ds(levels_sm[slot_of(step)], 1)
            rows_ref[step, 0:1, :] = 1.0 + held[0, row, :]
            rows_ref[step, 1:2, :] = held[1, row, :]
        modulated_ref[...] = modulated_rows(state_ref[...].astype(F32), rows_ref[0, 0:1, :], rows_ref[0, 1:2, :])
        for i, weight in enumerate((wk_out, wv_out)):
            total = None
            for j, part in enumerate(parts):
                weights[2 * i + j].wait()
                if i == 0 and j == 0:
                    weights[3].start()
                product = jnp.dot(modulated_ref[:, part], weight[part, :], preferred_element_type=F32)
                total = product if total is None else total + product
            out_ref[i] = head_normed(total, gain_columns(gain_ref, 1)) if i == 0 else total.astype(BF16)

    return pl.pallas_call(
        kernel,
        out_shape=(
            jax.ShapeDtypeStruct((half, depth), BF16),
            jax.ShapeDtypeStruct((2, half, width), BF16),
            jax.ShapeDtypeStruct((ITERS, 2, depth), F32),
            jax.ShapeDtypeStruct(wk.shape, BF16),
            jax.ShapeDtypeStruct(wv.shape, BF16),
        ),
        in_specs=[HBM] * 7,
        out_specs=(VMEM,) * 5,
        scratch_shapes=[
            pltpu.VMEM((2, *level_scale.shape), F32),
            pltpu.VMEM(state.shape, BF16),
            pltpu.VMEM(qk_gain.shape, F32),
            pltpu.SMEM(levels.shape, jnp.int32),
            pltpu.SemaphoreType.DMA((5,)),
            pltpu.SemaphoreType.DMA((4,)),
        ],
        compiler_params=params(8),
    )(*in_hbm(levels, level_scale, level_shift, state, qk_gain, wk, wv))


def updated(state, kept, received, size_row, fresh_row, noise):
    velocity = kept.astype(F32) + received.astype(F32)
    moved = state.astype(F32) + size_row * velocity
    return jnp.where(jnp.broadcast_to(fresh_row, moved.shape) > 0.5, noise.astype(F32), moved).astype(BF16)


def next_half(step, state, kept, received, control, noise, rows, qk_gain, wk, wv):
    half, depth = state.shape
    width = wk.shape[1]

    def kernel(state_ref, kept_ref, received_ref, control_ref, noise_ref, rows_ref, gain_ref, wk_ref, wv_ref, new_ref, modulated_ref, out_ref):
        new_ref[...] = updated(
            state_ref[...], kept_ref[...], received_ref[...], control_ref[0:1, :], control_ref[1:2, :], noise_ref[...]
        )
        modulated_ref[...] = modulated_rows(new_ref[...].astype(F32), rows_ref[step, 0:1, :], rows_ref[step, 1:2, :])
        project(modulated_ref[...], gain_ref, wk_ref, wv_ref, out_ref)

    return pl.pallas_call(
        kernel,
        out_shape=(
            jax.ShapeDtypeStruct((half, depth), BF16),
            jax.ShapeDtypeStruct((half, depth), BF16),
            jax.ShapeDtypeStruct((2, half, width), BF16),
        ),
        in_specs=[VMEM] * 9,
        out_specs=(VMEM,) * 3,
        compiler_params=params(8),
    )(state, kept, received, control, noise, rows, qk_gain, wk, wv)


def other_half(modulated, qk_gain, wk, wv, wq):
    half = modulated.shape[0]
    width = wk.shape[1]
    load = wq is not None

    def kernel(modulated_ref, gain_ref, wk_ref, wv_ref, *rest):
        out_ref = rest[load]
        if load:
            copy = pltpu.make_async_copy(rest[0], rest[2], rest[3])
            copy.start()
        project(modulated_ref[...], gain_ref, wk_ref, wv_ref, out_ref)
        if load:
            copy.wait()

    out = jax.ShapeDtypeStruct((2, half, width), BF16)
    return pl.pallas_call(
        kernel,
        out_shape=(out, jax.ShapeDtypeStruct(wq.shape, BF16)) if load else (out,),
        in_specs=[VMEM] * 4 + [HBM] * load,
        out_specs=(VMEM,) * (1 + load),
        scratch_shapes=[pltpu.SemaphoreType.DMA(())] * load,
        compiler_params=params(8),
    )(modulated, qk_gain, wk, wv, *(in_hbm(wq) if load else ()))


def attention_parts(query_pair, keys, values, bias):
    tokens = query_pair.shape[0]
    lane = lax.broadcasted_iota(jnp.int32, (tokens, LANES), 1)
    frame = lax.broadcasted_iota(jnp.int32, (tokens, LANES), 0) // (tokens // FRAMES)
    frame_of = (lane == frame).astype(BF16)
    first = lane < HD
    ones = jnp.ones((tokens, LANES), BF16)
    parts = []
    for which in (first, jnp.logical_not(first)):
        one = jnp.concatenate([jnp.where(which, query_pair, jnp.zeros_like(query_pair)), frame_of], axis=1)
        scores = lax.dot_general(
            one, jnp.concatenate([keys, bias], axis=1), (((1,), (1,)), ((), ())), preferred_element_type=F32
        )
        weights = jnp.exp2(scores).astype(BF16)
        parts.append(jnp.dot(weights, jnp.concatenate([values, ones], axis=1), preferred_element_type=F32))
    return (
        jnp.where(first, parts[0][:, :LANES], parts[1][:, :LANES]),
        jnp.where(first, parts[0][:, LANES:], parts[1][:, LANES:]),
    )


def pair_parts(query_ref, first_ref, second_ref, bias, columns):
    keys, values = (
        jnp.concatenate([first_ref[i, :, columns], second_ref[i, :, columns]], axis=0) for i in range(2)
    )
    return attention_parts(query_ref[:, columns], keys, values, bias)


def queries(step, mine, other, qk_gain, wq, pattern, own, own_other, levels, entry, step_size, fresh_noise, wo):
    half, depth = mine.shape
    tokens, width = 2 * half, wq.shape[1]
    scale = math.log2(math.e) / math.sqrt(HD)
    load = wo is not None

    def kernel(pattern_ref, levels_ref, entry_ref, size_ref, gain_ref, mine_ref, other_ref, wq_ref, own_ref, own_other_ref, noise_hbm, *rest):
        out_ref, bias_ref, sums_ref, control_ref, noise_ref = rest[load : load + 5]
        whole, sems = rest[-2:]
        copies = [pltpu.make_async_copy(noise_hbm.at[step], noise_ref, sems.at[0])]
        if load:
            copies.append(pltpu.make_async_copy(rest[0], rest[load + 5], sems.at[1]))
        for copy in copies:
            copy.start()
        fresh = slot_of(step + 1) == entry_ref[step]
        control_ref[0:1, :] = jnp.full((1, depth), size_ref[levels_ref[slot_of(step)]], F32)
        control_ref[1:2, :] = jnp.full((1, depth), jnp.where(fresh, 1.0, 0.0), F32)
        whole[:half, :] = mine_ref[...]
        whole[half:, :] = other_ref[...]
        window_bias(pattern_ref, bias_ref, slot_of(step), tokens // FRAMES)
        query = jnp.dot(whole[...], wq_ref[...], preferred_element_type=F32)
        out_ref[...] = head_normed(query, gain_columns(gain_ref, 0) * scale)
        for first in range(0, width, LANES):
            columns = slice(first, first + LANES)
            sums_ref[0, :, columns], sums_ref[1, :, columns] = pair_parts(out_ref, own_ref, own_other_ref, bias_ref[0], columns)
        for copy in copies:
            copy.wait()

    out_shape = [
        jax.ShapeDtypeStruct((tokens, width), BF16),
        jax.ShapeDtypeStruct((3, tokens, LANES), BF16),
        jax.ShapeDtypeStruct((2, tokens, width), F32),
        jax.ShapeDtypeStruct((2, depth), F32),
        jax.ShapeDtypeStruct((half, depth), BF16),
    ]
    if load:
        out_shape.append(jax.ShapeDtypeStruct(wo.shape, BF16))
    return pl.pallas_call(
        kernel,
        out_shape=out_shape,
        in_specs=[SMEM] * 4 + [VMEM] * 6 + [HBM] * (1 + load),
        out_specs=[VMEM] * (5 + load),
        scratch_shapes=[pltpu.VMEM((tokens, depth), BF16), pltpu.SemaphoreType.DMA((2,))],
        compiler_params=params(8),
    )(pattern, levels, entry, step_size, qk_gain, mine, other, wq, own, own_other, *in_hbm(fresh_noise), *(in_hbm(wo) if load else ()))


def attend(query, bias, sums, partner, neighbour):
    def kernel(query_ref, bias_ref, sums_ref, partner_ref, neighbour_ref, out_ref):
        for first in range(0, query_ref.shape[1], LANES):
            columns = slice(first, first + LANES)
            parts = pair_parts(query_ref, partner_ref, neighbour_ref, bias_ref[1], columns)
            for i in range(2):
                out_ref[i, :, columns] = sums_ref[i, :, columns] + parts[i]

    return pl.pallas_call(
        kernel,
        out_shape=jax.ShapeDtypeStruct(sums.shape, F32),
        in_specs=[VMEM] * 5,
        out_specs=VMEM,
        compiler_params=params(8),
    )(query, bias, sums, partner, neighbour)


def project_term(attended, wo_ref, rows, first, outs):
    for start in range(0, outs[0].shape[1], OUT_BLOCK):
        term = jnp.dot(
            attended[rows, :], wo_ref[:, first + start : first + start + OUT_BLOCK], preferred_element_type=F32
        ).astype(BF16)
        height = outs[0].shape[0]
        for i, out_ref in enumerate(outs):
            out_ref[:, start : start + OUT_BLOCK] = term[i * height : (i + 1) * height]


def attend_project(query, bias, sums, partner, neighbour, wo, both, width):
    tokens = query.shape[0]
    half = tokens // 2

    def kernel(query_ref, bias_ref, sums_ref, partner_ref, neighbour_ref, wo_ref, attended, *outs):
        for first in range(0, query_ref.shape[1], LANES):
            columns = slice(first, first + LANES)
            top, bottom = pair_parts(query_ref, partner_ref, neighbour_ref, bias_ref[2], columns)
            top = top + sums_ref[0, :, columns]
            bottom = bottom + sums_ref[1, :, columns]
            attended[:, columns] = (top / bottom).astype(BF16)
        project_term(attended, wo_ref, slice(0 if both else half, tokens), 0, outs)

    out = jax.ShapeDtypeStruct((half, width), BF16)
    return pl.pallas_call(
        kernel,
        out_shape=(jax.ShapeDtypeStruct(query.shape, BF16), *[out] * (1 + both)),
        in_specs=[VMEM] * 6,
        out_specs=(VMEM,) * (2 + both),
        compiler_params=params(8),
    )(query, bias, sums, partner, neighbour, wo)


def more_term(attended, wo, both, first, width):
    tokens = attended.shape[0]
    half = tokens // 2

    def kernel(attended_ref, wo_ref, *outs):
        project_term(attended_ref, wo_ref, slice(0, tokens if both else half), first, outs)

    out = jax.ShapeDtypeStruct((half, width), BF16)
    return pl.pallas_call(
        kernel,
        out_shape=(out,) * (1 + both),
        in_specs=[VMEM, VMEM],
        out_specs=(VMEM,) * (1 + both),
        compiler_params=params(8),
    )(attended, wo)


def last_update(state, first, kept, received, control, noise):
    columns = slice(first, first + kept.shape[1])

    def kernel(state_ref, kept_ref, received_ref, control_ref, noise_ref, out_ref):
        out_ref[...] = updated(
            state_ref[:, columns],
            kept_ref[...],
            received_ref[...],
            control_ref[0:1, columns],
            control_ref[1:2, columns],
            noise_ref[:, columns],
        )

    return pl.pallas_call(
        kernel,
        out_shape=jax.ShapeDtypeStruct(kept.shape, BF16),
        in_specs=[VMEM] * 5,
        out_specs=VMEM,
        compiler_params=params(8),
    )(state, kept, received, control, noise)


def exchanged(step, partner, block):
    count = lax.axis_size("queue")
    pairs = []
    for i in range(0 if partner else 1, count, 2):
        if (i + step) % count != count - 1:
            pairs += [(i, (i + 1) % count), ((i + 1) % count, i)]
    return lax.ppermute(block, "queue", pairs)


def on_device(
    latents, fresh_noise, levels, pattern, entry, level_scale, level_shift, step_size, qk_gain, wq, wk, wv, wo
):
    count = lax.axis_size("queue")
    state = latents[0]
    depth = state.shape[1]
    for step in range(ITERS):
        if step == 0:
            mine, own, rows, wk, wv = first_half(state, levels, level_scale, level_shift, qk_gain, wk, wv)
        else:
            state, mine, own = next_half(
                step, state, kept, received, control, noise, rows, qk_gain, wk, wv
            )
        other = swap_cores(mine)
        neighbour = exchanged(step, False, own)
        other, own = lax.optimization_barrier((other, own))
        theirs = exchanged(step, True, own), neighbour
        own_other, *loaded = other_half(other, qk_gain, wk, wv, wq if step == 0 else None)
        if loaded:
            wq = loaded[0]
        theirs_other = exchanged(step, True, own_other), exchanged(step, False, own_other)
        query, bias, sums, control, noise, *loaded = queries(
            step,
            mine,
            other,
            qk_gain,
            wq,
            pattern,
            own,
            own_other,
            levels,
            entry,
            step_size,
            fresh_noise,
            wo if step == 0 else None,
        )
        if loaded:
            wo = loaded[0]
        sums = attend(query, bias, sums, *theirs)
        if step < ITERS - 1:
            attended, sent = attend_project(query, bias, sums, *theirs_other, wo, False, depth)
            received = swap_cores(sent)
            (kept,) = more_term(attended, wo, False, 0, depth)
    width = depth // LAST_COLUMNS
    attended, *terms = attend_project(query, bias, sums, *theirs_other, wo, True, width)
    route = [(i, (i + ITERS) % count) for i in range(count)]
    result = []
    for first in range(0, depth, width):
        if first > 0:
            terms = more_term(attended, wo, True, first, width)
        part = last_update(state, first, terms[0], swap_cores(terms[1]), control, noise)
        result.append(lax.ppermute(part, "queue", route))
    return jnp.concatenate(result, axis=1)[None]


def solution(mesh):
    return jax.shard_map(
        on_device,
        mesh=mesh,
        in_specs=(
            P("queue", "seq", None),
            P(None, "seq", None),
            P(),
            P(),
            P(),
            P(),
            P(),
            P(),
            P(),
            P(None, "seq"),
            P(None, "seq"),
            P(None, "seq"),
            P("seq", None),
        ),
        out_specs=P("queue", "seq", None),
        check_vma=False,
    )
```

```python
import math

import jax
import jax.numpy as jnp
from jax import lax
from jax.experimental import pallas as pl
from jax.experimental.pallas import tpu as pltpu
from jax.sharding import PartitionSpec as P

HD = 64
FRAMES = 4
ITERS = 2
LANES = 128
EPS = 1e-06
CLOSED = -30000.0
BLOCK = 256
OUT_BLOCK = 768
LAST_COLUMNS = 2
MIB = 1 << 20
F32 = jnp.float32
BF16 = jnp.bfloat16

SMEM = pl.BlockSpec(memory_space=pltpu.SMEM)
VMEM = pl.BlockSpec(memory_space=pltpu.VMEM)
HBM = pl.BlockSpec(memory_space=pltpu.HBM)


def swap_cores(block):
    return lax.ppermute(block, "seq", [(0, 1), (1, 0)])


def in_hbm(*arrays):
    return tuple(pltpu.with_memory_space_constraint(array, pltpu.HBM) for array in arrays)


def params(mib):
    return pltpu.CompilerParams(vmem_limit_bytes=mib * MIB)


def slot_of(step):
    return lax.rem(lax.axis_index("queue") + step, lax.axis_size("queue"))


def modulated_rows(values, scale_row, shift_row):
    normed = values * lax.rsqrt(jnp.mean(values * values, axis=-1, keepdims=True) + EPS)
    return (normed * scale_row + shift_row).astype(BF16)


def head_normed(values, gain_row):
    rows, width = values.shape
    blocks = [values[:, first : first + BLOCK] for first in range(0, width, BLOCK)]
    stacked = jnp.concatenate(blocks, axis=0)
    row = lax.broadcasted_iota(jnp.int32, (BLOCK, BLOCK), 0)
    column = lax.broadcasted_iota(jnp.int32, (BLOCK, BLOCK), 1)
    same = (row // HD == column // HD).astype(BF16)
    sums = jnp.dot((stacked * stacked).astype(BF16), same, preferred_element_type=F32)
    normed = (stacked * lax.rsqrt(sums * (1.0 / HD) + EPS) * gain_row).astype(BF16)
    return jnp.concatenate([normed[i * rows : (i + 1) * rows] for i in range(len(blocks))], axis=1)


def gain_columns(gain_ref, which):
    return jnp.concatenate([gain_ref[which : which + 1, :]] * (BLOCK // HD), axis=1)


def window_bias(pattern_ref, bias_ref, slot, frame_rows):
    count, core = lax.axis_size("queue"), lax.axis_index("seq")
    odd = lax.rem(lax.axis_index("queue"), 2)
    lane = lax.broadcasted_iota(jnp.int32, (1, LANES), 1)
    half = FRAMES // 2
    for i, block in enumerate((1, 2 - 2 * odd, 2 * odd)):
        absent = slot == jnp.where(block == 0, 0, count - 1)
        for at in range(FRAMES):
            key_frame = lax.rem(at + half * core, FRAMES)
            row = jnp.zeros((1, LANES), F32)
            for f in range(FRAMES):
                if i == 0 and f == at:
                    continue
                closed = pattern_ref[lax.rem(f + half * core, FRAMES), block * FRAMES + key_frame] != 1
                if i > 0:
                    closed = jnp.logical_or(closed, absent)
                row = row + jnp.where(lane == f, jnp.where(closed, CLOSED, 0.0), 0.0)
            to, first = (0, at) if i == 0 else (1 + at // half, (i - 1) * half + at % half)
            rows = slice(first * frame_rows, (first + 1) * frame_rows)
            bias_ref[to, rows, :] = jnp.broadcast_to(row, (frame_rows, LANES)).astype(BF16)


def project(modulated, gain_ref, wk_ref, wv_ref, out_ref):
    keys = jnp.dot(modulated, wk_ref[...], preferred_element_type=F32)
    out_ref[0] = head_normed(keys, gain_columns(gain_ref, 1))
    out_ref[1] = jnp.dot(modulated, wv_ref[...], preferred_element_type=F32).astype(BF16)


def first_half(state, levels, level_scale, level_shift, qk_gain, wk, wv):
    half, depth = state.shape
    width = wk.shape[1]

    def kernel(levels_ref, scale_ref, shift_ref, state_hbm, gain_hbm, wk_ref, wv_ref, modulated_ref, out_ref, rows_ref, wk_out, wv_out, held, state_ref, gain_ref, levels_sm, sems, weight_sems):
        first = pltpu.make_async_copy(levels_ref, levels_sm, sems.at[0])
        first.start()
        tables = [
            pltpu.make_async_copy(scale_ref, held.at[0], sems.at[1]),
            pltpu.make_async_copy(shift_ref, held.at[1], sems.at[2]),
            pltpu.make_async_copy(state_hbm, state_ref, sems.at[3]),
            pltpu.make_async_copy(gain_hbm, gain_ref, sems.at[4]),
        ]
        parts = [pl.ds(0, depth // 2), pl.ds(depth // 2, depth // 2)]
        weights = [
            pltpu.make_async_copy(ref.at[part], out.at[part], weight_sems.at[2 * i + j])
            for i, (ref, out) in enumerate(((wk_ref, wk_out), (wv_ref, wv_out)))
            for j, part in enumerate(parts)
        ]
        for copy in tables + weights[:1]:
            copy.start()
        for copy in [first] + tables:
            copy.wait()
        for copy in weights[1:3]:
            copy.start()
        for step in range(ITERS):
            row = pl.ds(levels_sm[slot_of(step)], 1)
            rows_ref[step, 0:1, :] = 1.0 + held[0, row, :]
            rows_ref[step, 1:2, :] = held[1, row, :]
        modulated_ref[...] = modulated_rows(state_ref[...].astype(F32), rows_ref[0, 0:1, :], rows_ref[0, 1:2, :])
        for i, weight in enumerate((wk_out, wv_out)):
            total = None
            for j, part in enumerate(parts):
                weights[2 * i + j].wait()
                if i == 0 and j == 0:
                    weights[3].start()
                product = jnp.dot(modulated_ref[:, part], weight[part, :], preferred_element_type=F32)
                total = product if total is None else total + product
            out_ref[i] = head_normed(total, gain_columns(gain_ref, 1)) if i == 0 else total.astype(BF16)

    return pl.pallas_call(
        kernel,
        out_shape=(
            jax.ShapeDtypeStruct((half, depth), BF16),
            jax.ShapeDtypeStruct((2, half, width), BF16),
            jax.ShapeDtypeStruct((ITERS, 2, depth), F32),
            jax.ShapeDtypeStruct(wk.shape, BF16),
            jax.ShapeDtypeStruct(wv.shape, BF16),
        ),
        in_specs=[HBM] * 7,
        out_specs=(VMEM,) * 5,
        scratch_shapes=[
            pltpu.VMEM((2, *level_scale.shape), F32),
            pltpu.VMEM(state.shape, BF16),
            pltpu.VMEM(qk_gain.shape, F32),
            pltpu.SMEM(levels.shape, jnp.int32),
            pltpu.SemaphoreType.DMA((5,)),
            pltpu.SemaphoreType.DMA((4,)),
        ],
        compiler_params=params(8),
    )(*in_hbm(levels, level_scale, level_shift, state, qk_gain, wk, wv))


def updated(state, kept, received, size_row, fresh_row, noise):
    velocity = kept.astype(F32) + received.astype(F32)
    moved = state.astype(F32) + size_row * velocity
    return jnp.where(jnp.broadcast_to(fresh_row, moved.shape) > 0.5, noise.astype(F32), moved).astype(BF16)


def next_half(step, state, kept, received, control, noise, rows, qk_gain, wk, wv):
    half, depth = state.shape
    width = wk.shape[1]

    def kernel(state_ref, kept_ref, received_ref, control_ref, noise_ref, rows_ref, gain_ref, wk_ref, wv_ref, new_ref, modulated_ref, out_ref):
        new_ref[...] = updated(
            state_ref[...], kept_ref[...], received_ref[...], control_ref[0:1, :], control_ref[1:2, :], noise_ref[...]
        )
        modulated_ref[...] = modulated_rows(new_ref[...].astype(F32), rows_ref[step, 0:1, :], rows_ref[step, 1:2, :])
        project(modulated_ref[...], gain_ref, wk_ref, wv_ref, out_ref)

    return pl.pallas_call(
        kernel,
        out_shape=(
            jax.ShapeDtypeStruct((half, depth), BF16),
            jax.ShapeDtypeStruct((half, depth), BF16),
            jax.ShapeDtypeStruct((2, half, width), BF16),
        ),
        in_specs=[VMEM] * 9,
        out_specs=(VMEM,) * 3,
        compiler_params=params(8),
    )(state, kept, received, control, noise, rows, qk_gain, wk, wv)


def other_half(modulated, qk_gain, wk, wv, wq):
    half = modulated.shape[0]
    width = wk.shape[1]
    load = wq is not None

    def kernel(modulated_ref, gain_ref, wk_ref, wv_ref, *rest):
        out_ref = rest[load]
        if load:
            copy = pltpu.make_async_copy(rest[0], rest[2], rest[3])
            copy.start()
        project(modulated_ref[...], gain_ref, wk_ref, wv_ref, out_ref)
        if load:
            copy.wait()

    out = jax.ShapeDtypeStruct((2, half, width), BF16)
    return pl.pallas_call(
        kernel,
        out_shape=(out, jax.ShapeDtypeStruct(wq.shape, BF16)) if load else (out,),
        in_specs=[VMEM] * 4 + [HBM] * load,
        out_specs=(VMEM,) * (1 + load),
        scratch_shapes=[pltpu.SemaphoreType.DMA(())] * load,
        compiler_params=params(8),
    )(modulated, qk_gain, wk, wv, *(in_hbm(wq) if load else ()))


def attention_parts(query_pair, keys, values, bias):
    tokens = query_pair.shape[0]
    lane = lax.broadcasted_iota(jnp.int32, (tokens, LANES), 1)
    frame = lax.broadcasted_iota(jnp.int32, (tokens, LANES), 0) // (tokens // FRAMES)
    frame_of = (lane == frame).astype(BF16)
    first = lane < HD
    ones = jnp.ones((tokens, LANES), BF16)
    parts = []
    for which in (first, jnp.logical_not(first)):
        one = jnp.concatenate([jnp.where(which, query_pair, jnp.zeros_like(query_pair)), frame_of], axis=1)
        scores = lax.dot_general(
            one, jnp.concatenate([keys, bias], axis=1), (((1,), (1,)), ((), ())), preferred_element_type=F32
        )
        weights = jnp.exp2(scores).astype(BF16)
        parts.append(jnp.dot(weights, jnp.concatenate([values, ones], axis=1), preferred_element_type=F32))
    return (
        jnp.where(first, parts[0][:, :LANES], parts[1][:, :LANES]),
        jnp.where(first, parts[0][:, LANES:], parts[1][:, LANES:]),
    )


def pair_parts(query_ref, first_ref, second_ref, bias, columns):
    keys, values = (
        jnp.concatenate([first_ref[i, :, columns], second_ref[i, :, columns]], axis=0) for i in range(2)
    )
    return attention_parts(query_ref[:, columns], keys, values, bias)


def queries(step, mine, other, qk_gain, wq, pattern, own, own_other, levels, entry, step_size, fresh_noise, wo):
    half, depth = mine.shape
    tokens, width = 2 * half, wq.shape[1]
    scale = math.log2(math.e) / math.sqrt(HD)
    load = wo is not None

    def kernel(pattern_ref, levels_ref, entry_ref, size_ref, gain_ref, mine_ref, other_ref, wq_ref, own_ref, own_other_ref, noise_hbm, *rest):
        out_ref, bias_ref, sums_ref, control_ref, noise_ref = rest[load : load + 5]
        whole, sems = rest[-2:]
        copies = [pltpu.make_async_copy(noise_hbm.at[step], noise_ref, sems.at[0])]
        if load:
            copies.append(pltpu.make_async_copy(rest[0], rest[load + 5], sems.at[1]))
        for copy in copies:
            copy.start()
        fresh = slot_of(step + 1) == entry_ref[step]
        control_ref[0:1, :] = jnp.full((1, depth), size_ref[levels_ref[slot_of(step)]], F32)
        control_ref[1:2, :] = jnp.full((1, depth), jnp.where(fresh, 1.0, 0.0), F32)
        whole[:half, :] = mine_ref[...]
        whole[half:, :] = other_ref[...]
        window_bias(pattern_ref, bias_ref, slot_of(step), tokens // FRAMES)
        query = jnp.dot(whole[...], wq_ref[...], preferred_element_type=F32)
        out_ref[...] = head_normed(query, gain_columns(gain_ref, 0) * scale)
        for first in range(0, width, LANES):
            columns = slice(first, first + LANES)
            sums_ref[0, :, columns], sums_ref[1, :, columns] = pair_parts(out_ref, own_ref, own_other_ref, bias_ref[0], columns)
        for copy in copies:
            copy.wait()

    out_shape = [
        jax.ShapeDtypeStruct((tokens, width), BF16),
        jax.ShapeDtypeStruct((3, tokens, LANES), BF16),
        jax.ShapeDtypeStruct((2, tokens, width), F32),
        jax.ShapeDtypeStruct((2, depth), F32),
        jax.ShapeDtypeStruct((half, depth), BF16),
    ]
    if load:
        out_shape.append(jax.ShapeDtypeStruct(wo.shape, BF16))
    return pl.pallas_call(
        kernel,
        out_shape=out_shape,
        in_specs=[SMEM] * 4 + [VMEM] * 6 + [HBM] * (1 + load),
        out_specs=[VMEM] * (5 + load),
        scratch_shapes=[pltpu.VMEM((tokens, depth), BF16), pltpu.SemaphoreType.DMA((2,))],
        compiler_params=params(8),
    )(pattern, levels, entry, step_size, qk_gain, mine, other, wq, own, own_other, *in_hbm(fresh_noise), *(in_hbm(wo) if load else ()))


def attend(query, bias, sums, partner, neighbour):
    def kernel(query_ref, bias_ref, sums_ref, partner_ref, neighbour_ref, out_ref):
        for first in range(0, query_ref.shape[1], LANES):
            columns = slice(first, first + LANES)
            parts = pair_parts(query_ref, partner_ref, neighbour_ref, bias_ref[1], columns)
            for i in range(2):
                out_ref[i, :, columns] = sums_ref[i, :, columns] + parts[i]

    return pl.pallas_call(
        kernel,
        out_shape=jax.ShapeDtypeStruct(sums.shape, F32),
        in_specs=[VMEM] * 5,
        out_specs=VMEM,
        compiler_params=params(8),
    )(query, bias, sums, partner, neighbour)


def project_term(attended, wo_ref, rows, first, outs):
    for start in range(0, outs[0].shape[1], OUT_BLOCK):
        term = jnp.dot(
            attended[rows, :], wo_ref[:, first + start : first + start + OUT_BLOCK], preferred_element_type=F32
        ).astype(BF16)
        height = outs[0].shape[0]
        for i, out_ref in enumerate(outs):
            out_ref[:, start : start + OUT_BLOCK] = term[i * height : (i + 1) * height]


def attend_project(query, bias, sums, partner, neighbour, wo, both, width):
    tokens = query.shape[0]
    half = tokens // 2

    def kernel(query_ref, bias_ref, sums_ref, partner_ref, neighbour_ref, wo_ref, attended, *outs):
        for first in range(0, query_ref.shape[1], LANES):
            columns = slice(first, first + LANES)
            top, bottom = pair_parts(query_ref, partner_ref, neighbour_ref, bias_ref[2], columns)
            top = top + sums_ref[0, :, columns]
            bottom = bottom + sums_ref[1, :, columns]
            attended[:, columns] = (top / bottom).astype(BF16)
        project_term(attended, wo_ref, slice(0 if both else half, tokens), 0, outs)

    out = jax.ShapeDtypeStruct((half, width), BF16)
    return pl.pallas_call(
        kernel,
        out_shape=(jax.ShapeDtypeStruct(query.shape, BF16), *[out] * (1 + both)),
        in_specs=[VMEM] * 6,
        out_specs=(VMEM,) * (2 + both),
        compiler_params=params(8),
    )(query, bias, sums, partner, neighbour, wo)


def more_term(attended, wo, both, first, width):
    tokens = attended.shape[0]
    half = tokens // 2

    def kernel(attended_ref, wo_ref, *outs):
        project_term(attended_ref, wo_ref, slice(0, tokens if both else half), first, outs)

    out = jax.ShapeDtypeStruct((half, width), BF16)
    return pl.pallas_call(
        kernel,
        out_shape=(out,) * (1 + both),
        in_specs=[VMEM, VMEM],
        out_specs=(VMEM,) * (1 + both),
        compiler_params=params(8),
    )(attended, wo)


def last_update(state, first, kept, received, control, noise):
    columns = slice(first, first + kept.shape[1])

    def kernel(state_ref, kept_ref, received_ref, control_ref, noise_ref, out_ref):
        out_ref[...] = updated(
            state_ref[:, columns],
            kept_ref[...],
            received_ref[...],
            control_ref[0:1, columns],
            control_ref[1:2, columns],
            noise_ref[:, columns],
        )

    return pl.pallas_call(
        kernel,
        out_shape=jax.ShapeDtypeStruct(kept.shape, BF16),
        in_specs=[VMEM] * 5,
        out_specs=VMEM,
        compiler_params=params(8),
    )(state, kept, received, control, noise)


def exchanged(step, partner, block):
    count = lax.axis_size("queue")
    pairs = []
    for i in range(0 if partner else 1, count, 2):
        if (i + step) % count != count - 1:
            pairs += [(i, (i + 1) % count), ((i + 1) % count, i)]
    return lax.ppermute(block, "queue", pairs)


def on_device(
    latents, fresh_noise, levels, pattern, entry, level_scale, level_shift, step_size, qk_gain, wq, wk, wv, wo
):
    count = lax.axis_size("queue")
    state = latents[0]
    depth = state.shape[1]
    for step in range(ITERS):
        if step == 0:
            mine, own, rows, wk, wv = first_half(state, levels, level_scale, level_shift, qk_gain, wk, wv)
        else:
            state, mine, own = next_half(
                step, state, kept, received, control, noise, rows, qk_gain, wk, wv
            )
        other = swap_cores(mine)
        neighbour = exchanged(step, False, own)
        other, own = lax.optimization_barrier((other, own))
        theirs = exchanged(step, True, own), neighbour
        own_other, *loaded = other_half(other, qk_gain, wk, wv, wq if step == 0 else None)
        if loaded:
            wq = loaded[0]
        theirs_other = exchanged(step, True, own_other), exchanged(step, False, own_other)
        query, bias, sums, control, noise, *loaded = queries(
            step,
            mine,
            other,
            qk_gain,
            wq,
            pattern,
            own,
            own_other,
            levels,
            entry,
            step_size,
            fresh_noise,
            wo if step == 0 else None,
        )
        if loaded:
            wo = loaded[0]
        sums = attend(query, bias, sums, *theirs)
        if step < ITERS - 1:
            attended, sent = attend_project(query, bias, sums, *theirs_other, wo, False, depth)
            received = swap_cores(sent)
            (kept,) = more_term(attended, wo, False, 0, depth)
    width = depth // LAST_COLUMNS
    attended, *terms = attend_project(query, bias, sums, *theirs_other, wo, True, width)
    route = [(i, (i + ITERS) % count) for i in range(count)]
    result = []
    for first in range(0, depth, width):
        if first > 0:
            terms = more_term(attended, wo, True, first, width)
        part = last_update(state, first, terms[0], swap_cores(terms[1]), control, noise)
        result.append(lax.ppermute(part, "queue", route))
    return jnp.concatenate(result, axis=1)[None]


def solution(mesh):
    return jax.shard_map(
        on_device,
        mesh=mesh,
        in_specs=(
            P("queue", "seq", None),
            P(None, "seq", None),
            P(),
            P(),
            P(),
            P(),
            P(),
            P(),
            P(),
            P(None, "seq"),
            P(None, "seq"),
            P(None, "seq"),
            P("seq", None),
        ),
        out_specs=P("queue", "seq", None),
        check_vma=False,
    )
```
